32 devices in a mesh: expert: 8 (over y, x, core), dp: 4 (over z).
Axes of the slice: x: 2, y: 2, z: 4, core: 2. Of those that a mesh axis runs over, the one named last changes fastest.
Arguments:
- attn_rows: bfloat16 [4096, 7168], P('dp', 'expert'), may hold values from -6 to 6
- out_grad: bfloat16 [4096, 7168], P('dp', 'expert'), may hold values from -6 to 6
- routes: int32 [4096, 8], P(('dp', 'expert')), may hold values from 0 to 255, as said below
- gates: bfloat16 [4096, 8], P(('dp', 'expert')), may hold values from 0.049804688 to 0.5
- w_gate: bfloat16 [8, 7168, 2048], P('expert', None, 'dp'), may hold values from -0.0625 to 0.0625
- w_up: bfloat16 [8, 7168, 2048], P('expert', None, 'dp'), may hold values from -0.0625 to 0.0625
- w_down: bfloat16 [8, 2048, 7168], P('expert', 'dp'), may hold values from -0.125 to 0.125
Outputs:
- grad_input: bfloat16 [4096, 7168], P('dp', 'expert')
- grad_w_gate: bfloat16 [8, 7168, 2048], P('expert', None, 'dp')
- grad_w_up: bfloat16 [8, 7168, 2048], P('expert', None, 'dp')
The draws below stay inside these ranges and needn't reach their ends.
Inputs may be any that keep to these rules, and one draw needn't show every extreme that they name: `routes`: each row names 8 different experts. In the 128 rows of one device (aligned blocks of 128 rows) no window expert (below 8) is named by more than 6 rows; in every device's rows some window expert is named by exactly 6 rows, and one window expert is named by exactly 6 rows of every device.
All inputs are finite; a program needn't handle non-finite values.
Results may differ from the reference program's by a relative error of at most 0.0058.
Values may be sent and summed in bfloat16 or wider, within the bound.
No kernel may reach another device: no remote copies, remote signals or barrier semaphores. Data moves between devices by JAX's collectives and lax.ppermute only.
A program may use at most 256 MiB of HBM per device.

```python
import math
import jax
import jax.numpy as jnp
from jax import lax

D = 7168
FF = 2048
TOP = 8
ROUTED = 256
TOK_DEV = 128
EXPERTS = 8
TOKENS = 4096
CAP = 6
EXPERT_ROWS = 192
N_DP = 4


def draw_routes(key, part):
    blocks = TOKENS // TOK_DEV
    keys = jax.random.split(jax.random.fold_in(key, 17), 6)
    expert_ids = jnp.arange(EXPERTS, dtype=jnp.int32)
    level = (2 ** jax.random.randint(keys[0], (EXPERTS,), 0, 4)).astype(jnp.int32)
    top_load = level * CAP // 4 + 1
    counts = jax.random.randint(keys[1], (blocks, EXPERTS), 0, 1 << 20).astype(jnp.int32) % top_load[None, :]
    counts = jnp.minimum(counts, CAP).astype(jnp.int32)
    steady = jax.random.randint(keys[2], (), 0, EXPERTS).astype(jnp.int32)
    moving = jax.random.randint(keys[3], (blocks,), 0, EXPERTS).astype(jnp.int32)
    forced = (expert_ids[None, :] == steady) | (expert_ids[None, :] == moving[:, None])
    counts = jnp.where(forced, CAP, counts).astype(jnp.int32)
    slot_ids = jnp.arange(CAP, dtype=jnp.int32)
    active = (slot_ids[None, None, :] < counts[:, :, None]).reshape(blocks, EXPERTS * CAP).astype(jnp.int32)
    rank = (jnp.cumsum(active, axis=1) - active).astype(jnp.int32)
    orders = jax.vmap(lambda sub: jax.random.permutation(sub, TOK_DEV))(jax.random.split(keys[4], blocks)).astype(jnp.int32)
    row_pos = rank % TOK_DEV
    slot_pos = rank // TOK_DEV
    row_of = jnp.take_along_axis(orders, row_pos, axis=1).astype(jnp.int32)
    row_of = jnp.where(active > 0, row_of, TOK_DEV).astype(jnp.int32)
    named = jnp.broadcast_to(jnp.repeat(expert_ids, CAP)[None, :], (blocks, EXPERTS * CAP))
    block_ids = jnp.broadcast_to(jnp.arange(blocks, dtype=jnp.int32)[:, None], (blocks, EXPERTS * CAP))
    table = jnp.full((blocks, TOK_DEV, TOP), -1, jnp.int32)
    table = table.at[block_ids, row_of, slot_pos].set(named, mode='drop')
    table = table.reshape(TOKENS, TOP)
    outside = ROUTED - EXPERTS
    scores = jax.random.randint(keys[5], (TOKENS, outside), 0, 1 << 20).astype(jnp.int32) * outside + jnp.arange(outside, dtype=jnp.int32)[None, :]
    unused, chosen = lax.top_k(scores, TOP)
    return jnp.where(table >= 0, table, EXPERTS + chosen.astype(jnp.int32)).astype(jnp.int32)


def steps_of(key, extent, shards, smallest, top_value):
    level = 1.0
    for dim, blocks in shards:
        steps = jax.random.uniform(jax.random.fold_in(jax.random.fold_in(key, 6), dim), (blocks,), jnp.float32, smallest / len(shards), top_value / len(shards))
        level = level * jnp.repeat(jnp.exp(steps), extent[dim] // blocks).reshape((-1,) + (1,) * (len(extent) - 1 - dim))
    return level


def gaussian(stream_key, extent, spread, reach, shards=(), kind=jnp.bfloat16):
    entries = spread * jax.random.normal(stream_key, extent, jnp.float32)
    if shards:
        entries = entries * steps_of(stream_key, extent, shards, -0.22, 0.18)
    return jnp.clip(entries, -reach, reach).astype(kind)


def setup_inputs(seed: int = 0) -> dict:
    key_list = jax.random.split(jax.random.key(seed), 8)
    return {
        "attn_rows": gaussian(key_list[0], (TOKENS, D), 1.0, 6.0, ((0, 4), (1, 8))),
        "out_grad": gaussian(key_list[1], (TOKENS, D), 1.0, 6.0, ((0, 4), (1, 8))),
        "routes": draw_routes(jax.random.fold_in(key_list[7], 71), 0),
        "gates": jnp.clip(jnp.exp(math.log(0.5) - 2.306499 * jax.random.uniform(key_list[3], (TOKENS, TOP), jnp.float32) ** steps_of(key_list[3], (TOKENS, TOP), ((0, 32),), -0.2, 0.2)), 0.049804688, 0.5).astype(jnp.bfloat16),
        "w_gate": gaussian(key_list[4], (EXPERTS, D, FF), D ** -0.5, 0.0625, ((0, 8), (2, 4))),
        "w_up": gaussian(key_list[5], (EXPERTS, D, FF), D ** -0.5, 0.0625, ((0, 8), (2, 4))),
        "w_down": gaussian(key_list[6], (EXPERTS, FF, D), FF ** -0.5, 0.125, ((0, 8), (1, 4))),
    }


def reference(attn_rows, out_grad, routes, gates, w_gate, w_up, w_down):
    expert_ids = jnp.arange(EXPERTS, dtype=jnp.int32)
    gate_full = gates.astype(jnp.float32)
    slices = FF // N_DP

    def one_expert(carry, items):
        expert_id, gate_mat, up_mat, down_mat = items
        routed = jnp.any(routes == expert_id, axis=1)
        picked = jnp.argsort(jnp.where(routed, 0, 1).astype(jnp.int32), stable=True)[:EXPERT_ROWS].astype(jnp.int32)
        coef_all = jnp.sum(jnp.where(routes == expert_id, gate_full, jnp.zeros_like(gate_full)), axis=1)
        coef = coef_all[picked]
        token_rows = attn_rows[picked]
        grad_rows = out_grad[picked]
        gate_pre = jnp.dot(token_rows, gate_mat, preferred_element_type=jnp.float32)
        up_proj = jnp.dot(token_rows, up_mat, preferred_element_type=jnp.float32)
        sigma_gate = jax.nn.sigmoid(gate_pre)
        activated = gate_pre * sigma_gate
        back_proj = jnp.dot(grad_rows, down_mat.T, preferred_element_type=jnp.float32)
        grad_hidden = coef[:, None] * back_proj
        grad_gate = (grad_hidden * up_proj * sigma_gate * (1.0 + gate_pre * (1.0 - sigma_gate))).astype(jnp.bfloat16)
        grad_up = (grad_hidden * activated).astype(jnp.bfloat16)
        g_gate = jnp.dot(token_rows.T, grad_gate, preferred_element_type=jnp.float32).astype(jnp.bfloat16)
        g_up = jnp.dot(token_rows.T, grad_up, preferred_element_type=jnp.float32).astype(jnp.bfloat16)
        left_gate = grad_gate.astype(jnp.float32).reshape(EXPERT_ROWS, N_DP, slices)
        left_up = grad_up.astype(jnp.float32).reshape(EXPERT_ROWS, N_DP, slices)
        right_gate = gate_mat.astype(jnp.float32).reshape(D, N_DP, slices)
        right_up = up_mat.astype(jnp.float32).reshape(D, N_DP, slices)
        pieces = jnp.einsum("tsf,dsf->tsd", left_gate, right_gate) + jnp.einsum("tsf,dsf->tsd", left_up, right_up)
        pieces = lax.optimization_barrier(pieces.astype(jnp.bfloat16)).astype(jnp.float32)
        contribution = jnp.sum(pieces, axis=1)
        carry = carry.at[picked].add(contribution)
        return carry, (g_gate, g_up)

    total, grads = lax.scan(one_expert, jnp.zeros((TOKENS, D), jnp.float32), (expert_ids, w_gate, w_up, w_down))
    return (total.astype(jnp.bfloat16), grads[0], grads[1])
```

```python
import functools
import math

import jax
import jax.numpy as jnp
from jax import lax
from jax.experimental import pallas as pl
from jax.experimental.pallas import tpu as pltpu
from jax.sharding import PartitionSpec as P

BF = jnp.bfloat16
F32 = jnp.float32
VMEM_LIMIT = 48 * 1024 * 1024
ROWS_DIMS = (((1,), (1,)), ((), ()))
FIRST_DIMS = (((0,), (0,)), ((), ()))


def params(*semantics):
    return pltpu.CompilerParams(
        vmem_limit_bytes=VMEM_LIMIT, dimension_semantics=semantics or None
    )


def cost(flops, moved):
    return pl.CostEstimate(flops=int(flops), bytes_accessed=int(moved), transcendentals=0)


def compact_kernel(dims, table_ref, x_ref, dy_ref, x1, d1, x2, d2, gates_ref, onehot_ref):
    experts, blocks, own, top, first, second = dims
    tokens = blocks * own
    table = table_ref[...].astype(F32)
    ids = lax.broadcasted_iota(jnp.int32, (experts, 1), 0).astype(F32)
    match = jnp.zeros((experts, tokens), F32)
    weight = jnp.zeros((experts, tokens), F32)
    for k in range(top):
        hit = table[k : k + 1, :] == ids
        match = match + jnp.where(hit, 1.0, 0.0)
        weight = weight + jnp.where(hit, table[top + k : top + k + 1, :], 0.0)
    earlier = (
        lax.broadcasted_iota(jnp.int32, (own, own), 0)
        < lax.broadcasted_iota(jnp.int32, (own, own), 1)
    )
    earlier = jnp.where(earlier, 1.0, 0.0).astype(BF)
    codes = []
    for b in range(blocks):
        part = match[:, b * own : (b + 1) * own]
        rank = jnp.dot(part.astype(BF), earlier, preferred_element_type=F32)
        codes.append(jnp.where(part > 0.0, rank * blocks + b, -1.0))
    code = jnp.concatenate(codes, axis=1)
    slots = lax.broadcasted_iota(jnp.int32, (first + second, 1), 0).astype(F32)
    for e in range(experts):
        placed = jnp.where(slots == code[e : e + 1, :], 1.0, 0.0)
        coef = jnp.sum(placed * weight[e : e + 1, :], axis=1, keepdims=True)
        gates_ref[e] = jnp.broadcast_to(coef, (first + second, 128)).astype(BF)
        placed = placed.astype(BF)
        onehot_ref[e * first : (e + 1) * first, :] = placed[:first]
        start = experts * first + e * second
        onehot_ref[start : start + second, :] = placed[first:]
    split = experts * first
    for src, one, two in ((x_ref, x1, x2), (dy_ref, d1, d2)):
        rows = jnp.dot(onehot_ref[...], src[...], preferred_element_type=F32).astype(BF)
        one[...] = rows[:split].reshape(one.shape)
        two[...] = rows[split:].reshape(two.shape)


def compact(table, x, dy, experts, blocks, own, first, second):
    top = table.shape[0] // 2
    feat = x.shape[1]
    rows = experts * (first + second)
    tokens = blocks * own
    big = jax.ShapeDtypeStruct((experts, first, feat), BF)
    small = jax.ShapeDtypeStruct((experts, second, feat), BF)
    return pl.pallas_call(
        functools.partial(compact_kernel, (experts, blocks, own, top, first, second)),
        out_shape=(
            big,
            big,
            small,
            small,
            jax.ShapeDtypeStruct((experts, first + second, 128), BF),
            jax.ShapeDtypeStruct((rows, tokens), BF),
        ),
        compiler_params=params(),
        cost_estimate=cost(4 * rows * tokens * feat, 4 * tokens * feat + 4 * rows * feat),
        name="compact",
    )(table, x, dy)


def up_kernel(slots, *refs):
    x, (w_gate, w_up, gate_pre, up_proj) = refs[:slots], refs[slots:]
    rows = jnp.concatenate([r[0] for r in x], axis=0)

    @pl.when(pl.program_id(0) == 0)
    def _():
        gate_pre[...] = jnp.zeros_like(gate_pre)
        up_proj[...] = jnp.zeros_like(up_proj)

    gate_pre[...] += jnp.dot(rows, w_gate[0], preferred_element_type=F32)
    up_proj[...] += jnp.dot(rows, w_up[0], preferred_element_type=F32)


def up(x, w_gate, w_up):
    pieces, rows, feat = x[0].shape
    hidden = w_gate.shape[2]
    total = len(x) * rows
    x_spec = pl.BlockSpec((1, rows, feat), lambda f: (f, 0, 0))
    w_spec = pl.BlockSpec((1, feat, hidden), lambda f: (0, f, 0))
    o_spec = pl.BlockSpec((total, hidden), lambda f: (0, 0))
    out = jax.ShapeDtypeStruct((total, hidden), F32)
    return pl.pallas_call(
        functools.partial(up_kernel, len(x)),
        grid=(pieces,),
        in_specs=[x_spec] * len(x) + [w_spec] * 2,
        out_specs=(o_spec, o_spec),
        out_shape=(out, out),
        compiler_params=params("arbitrary"),
        cost_estimate=cost(4 * total * pieces * feat * hidden, 4 * pieces * feat * hidden),
        name="up",
    )(*x, w_gate, w_up)


def hidden_kernel(slots, start, origin, *refs):
    dy, (w_down, gates, gate_pre, up_proj, grad_gate, grad_up, acc) = refs[:slots], refs[slots:]
    rows = jnp.concatenate([r[0] for r in dy], axis=0)
    count = dy[0].shape[1]

    @pl.when(pl.program_id(0) == 0)
    def _():
        acc[...] = jnp.zeros_like(acc)

    acc[...] += lax.dot_general(rows, w_down[0], ROWS_DIMS, preferred_element_type=F32)

    @pl.when(pl.program_id(0) == pl.num_programs(0) - 1)
    def _():
        coef = jnp.concatenate(
            [gates[origin[k], start : start + count, :1] for k in range(slots)], axis=0
        )
        pre = gate_pre[...]
        sigma = jax.nn.sigmoid(pre)
        grad_hidden = coef.astype(F32) * acc[...]
        grad_gate[...] = (
            grad_hidden * up_proj[...] * sigma * (1.0 + pre * (1.0 - sigma))
        ).astype(BF)
        grad_up[...] = (grad_hidden * (pre * sigma)).astype(BF)


def hidden_grads(dy, w_down, gates, origin, start, gate_pre, up_proj):
    pieces, rows, feat = dy[0].shape
    hidden = w_down.shape[1]
    total = len(dy) * rows
    whole = lambda shape: pl.BlockSpec(shape, lambda f, o: (0,) * len(shape))
    out = jax.ShapeDtypeStruct((total, hidden), BF)
    return pl.pallas_call(
        functools.partial(hidden_kernel, len(dy), start),
        grid_spec=pltpu.PrefetchScalarGridSpec(
            num_scalar_prefetch=1,
            grid=(pieces,),
            in_specs=[pl.BlockSpec((1, rows, feat), lambda f, o: (f, 0, 0))] * len(dy)
            + [
                pl.BlockSpec((1, hidden, feat), lambda f, o: (0, 0, f)),
                whole(gates.shape),
                whole((total, hidden)),
                whole((total, hidden)),
            ],
            out_specs=(whole((total, hidden)), whole((total, hidden))),
            scratch_shapes=[pltpu.VMEM((total, hidden), F32)],
        ),
        out_shape=(out, out),
        compiler_params=params("arbitrary"),
        cost_estimate=cost(2 * total * pieces * feat * hidden, 2 * pieces * feat * hidden),
        name="hidden_grads",
    )(origin, *dy, w_down, gates, gate_pre, up_proj)


def back_kernel(grad_gate, grad_up, w_gate, w_up, *outs):
    value = lax.dot_general(grad_gate[...], w_gate[0], ROWS_DIMS, preferred_element_type=F32)
    value += lax.dot_general(grad_up[...], w_up[0], ROWS_DIMS, preferred_element_type=F32)
    rows = outs[0].shape[1]
    for k, out in enumerate(outs):
        out[0] = value[k * rows : (k + 1) * rows].astype(BF)


def back(grad_gate, grad_up, w_gate, w_up, slots, pieces):
    total, hidden = grad_gate.shape
    rows = total // slots
    feat = w_gate.shape[1] // pieces
    g_spec = pl.BlockSpec((total, hidden), lambda f: (0, 0))
    w_spec = pl.BlockSpec((1, feat, hidden), lambda f: (0, f, 0))
    return pl.pallas_call(
        back_kernel,
        grid=(pieces,),
        in_specs=[g_spec, g_spec, w_spec, w_spec],
        out_specs=[pl.BlockSpec((1, rows, feat), lambda f: (f, 0, 0))] * slots,
        out_shape=[jax.ShapeDtypeStruct((pieces, rows, feat), BF)] * slots,
        compiler_params=params("arbitrary"),
        cost_estimate=cost(4 * total * pieces * feat * hidden, 4 * pieces * feat * hidden),
        name="back",
    )(grad_gate, grad_up, w_gate, w_up)


def weights_kernel(slots, *refs):
    x, (gates, ups, g_gate, g_up) = refs[:slots], refs[slots:]
    rows = jnp.concatenate([r[0] for r in x], axis=0)
    g_gate[0] = lax.dot_general(rows, gates[...], FIRST_DIMS, preferred_element_type=F32).astype(BF)
    g_up[0] = lax.dot_general(rows, ups[...], FIRST_DIMS, preferred_element_type=F32).astype(BF)


def weight_grads(x, grad_gate, grad_up):
    pieces, _, feat = x[0].shape
    total, hidden = grad_gate.shape
    g_spec = pl.BlockSpec((total, hidden), lambda f: (0, 0))
    o_spec = pl.BlockSpec((1, feat, hidden), lambda f: (0, f, 0))
    out = jax.ShapeDtypeStruct((1, pieces * feat, hidden), BF)
    return pl.pallas_call(
        functools.partial(weights_kernel, len(x)),
        grid=(pieces,),
        in_specs=[pl.BlockSpec((1,) + v.shape[1:], lambda f: (f, 0, 0)) for v in x]
        + [g_spec, g_spec],
        out_specs=(o_spec, o_spec),
        out_shape=(out, out),
        compiler_params=params("arbitrary"),
        cost_estimate=cost(4 * total * pieces * feat * hidden, 4 * pieces * feat * hidden),
        name="weight_grads",
    )(*x, grad_gate, grad_up)


def scatter_kernel(onehot, one, two, out):
    split = one.shape[0]
    value = lax.dot_general(onehot[:split, :], one[...], FIRST_DIMS, preferred_element_type=F32)
    value += lax.dot_general(onehot[split:, :], two[...], FIRST_DIMS, preferred_element_type=F32)
    out[...] = value.astype(BF)


def scatter(onehot, one, two):
    rows, tokens = onehot.shape
    feat = one.shape[1]
    return pl.pallas_call(
        scatter_kernel,
        out_shape=jax.ShapeDtypeStruct((tokens, feat), BF),
        compiler_params=params(),
        cost_estimate=cost(2 * rows * tokens * feat, 2 * rows * tokens + 4 * tokens * feat),
        name="scatter",
    )(onehot, one, two)


def line_steps(n):
    right = {s: [(i, i + 1) for i in range(s - 1, n - 1)] for s in range(1, n)}
    left = {s: [(i, i - 1) for i in range(1, n - s + 1)] for s in range(1, n)}
    return right, left


def gather_line(arrays):
    n = lax.axis_size("dp")
    me = lax.axis_index("dp")
    right, left = line_steps(n)
    from_left = [{0: a} for a in arrays]
    from_right = [{0: a} for a in arrays]
    for s in range(1, n):
        for r, l in zip(from_left, from_right):
            r[s] = lax.ppermute(r[s - 1], "dp", right[s])
            l[s] = lax.ppermute(l[s - 1], "dp", left[s])
    return [
        [a] + [jnp.where(me >= k, r[k], l[n - k]) for k in range(1, n)]
        for a, r, l in zip(arrays, from_left, from_right)
    ]


def add(*values):
    total = values[0].astype(F32)
    for v in values[1:]:
        total = total + v.astype(F32)
    return total.astype(BF)


def sum_line(slots):
    n = len(slots)
    got_r, got_l = [], []
    for s in range(1, n):
        out_r = add(slots[s], *got_r)
        out_l = add(slots[n - s], *got_l)
        got_r = [lax.ppermute(out_r, "dp", [(i, i + 1) for i in range(s)])]
        got_l = [lax.ppermute(out_l, "dp", [(i, i - 1) for i in range(n - s, n)])]
    return add(slots[0], *got_r, *got_l)


def widen(values, fold):
    if fold == 1:
        return values
    pieces, rows, feat = values.shape
    values = values.reshape(pieces // fold, fold, rows, feat)
    return jnp.swapaxes(values, 1, 2).reshape(pieces // fold, rows, fold * feat)


def narrow(values, fold):
    if fold == 1:
        return values
    pieces, rows, feat = values.shape
    values = values.reshape(pieces, rows, fold, feat // fold)
    return jnp.swapaxes(values, 1, 2).reshape(pieces * fold, rows, feat // fold)


def per_device(attn_rows, out_grad, routes, gates, w_gate, w_up, w_down):
    experts = lax.axis_size("expert")
    groups = lax.axis_size("dp")
    own, top = routes.shape
    feat = attn_rows.shape[1]
    capacity = 3 * own // 64
    late = capacity // 3
    first, second = (capacity - late) * experts, late * experts
    fold = 128 // math.gcd(feat, 128)
    pieces = experts // fold

    named = jnp.minimum(routes, experts).astype(BF)
    table = lax.all_gather(jnp.concatenate([named, gates], axis=1), "expert", axis=0, tiled=True)
    x1, d1, x2, d2, coef, onehot = compact(
        table.T, attn_rows, out_grad, experts, experts, own, first, second
    )

    def exchange(values):
        return lax.all_to_all(values, "expert", split_axis=0, concat_axis=0, tiled=True)

    x1, d1, x2, d2 = exchange(x1), exchange(d1), exchange(x2), exchange(d2)
    own_coef = lax.dynamic_index_in_dim(coef, lax.axis_index("expert"), 0, keepdims=False)
    all_coef = lax.all_gather(own_coef, "dp", axis=0)
    origin = lax.rem(
        lax.axis_index("dp") + groups - jnp.arange(groups, dtype=jnp.int32), groups
    ).astype(jnp.int32)

    x1s, d1s = gather_line([x1, d1])
    x2s, d2s = gather_line([x2, d2])
    x1s, d1s, x2s, d2s = [[widen(v, fold) for v in s] for s in (x1s, d1s, x2s, d2s)]

    def chunk(xs, ds, start):
        gate_pre, up_proj = up(xs, w_gate, w_up)
        grad_gate, grad_up = hidden_grads(ds, w_down, all_coef, origin, start, gate_pre, up_proj)
        parts = back(grad_gate, grad_up, w_gate, w_up, groups, pieces)
        summed = exchange(sum_line([narrow(v, fold) for v in parts]))
        return summed.reshape(-1, feat), grad_gate, grad_up

    sum1, gg1, gu1 = chunk(x1s, d1s, 0)
    sum2, gg2, gu2 = chunk(x2s, d2s, first)
    g_gate, g_up = weight_grads(
        x1s + x2s, jnp.concatenate([gg1, gg2], axis=0), jnp.concatenate([gu1, gu2], axis=0)
    )
    return scatter(onehot, sum1, sum2), g_gate, g_up


def solution(mesh):
    return jax.shard_map(
        per_device,
        mesh=mesh,
        in_specs=(
            P("dp", "expert"),
            P("dp", "expert"),
            P(("dp", "expert"), None),
            P(("dp", "expert"), None),
            P("expert", None, "dp"),
            P("expert", None, "dp"),
            P("expert", "dp", None),
        ),
        out_specs=(P("dp", "expert"), P("expert", None, "dp"), P("expert", None, "dp")),
        check_vma=False,
    )
```

```python
import functools
import math

import jax
import jax.numpy as jnp
from jax import lax
from jax.experimental import pallas as pl
from jax.experimental.pallas import tpu as pltpu
from jax.sharding import PartitionSpec as P

BF = jnp.bfloat16
F32 = jnp.float32
VMEM_LIMIT = 58 * 1024 * 1024
TILE = 16
AHEAD = 3
ROWS_DIMS = (((1,), (1,)), ((), ()))
FIRST_DIMS = (((0,), (0,)), ((), ()))


def params(*semantics):
    return pltpu.CompilerParams(
        vmem_limit_bytes=VMEM_LIMIT, dimension_semantics=semantics or None
    )


def cost(flops, moved):
    return pl.CostEstimate(flops=int(flops), bytes_accessed=int(moved), transcendentals=0)


def label_kernel(experts, routes, gates, out):
    top = routes.shape[0]
    out[:top, :] = jnp.minimum(routes[...], experts).astype(F32).astype(BF)
    out[top:, :] = gates[...]


def label(routes, gates, experts):
    top, tokens = routes.shape
    return pl.pallas_call(
        functools.partial(label_kernel, experts),
        out_shape=jax.ShapeDtypeStruct((2 * top, tokens), BF),
        name="label",
    )(routes, gates)


def compact_kernel(
    experts, table, x_hbm, dy_hbm, x_out, dy_out, gates, onehot, x_buf, dy_buf, sems
):
    blocks, labels, own = table.shape
    top = labels // 2
    loads = [
        pltpu.make_async_copy(x_hbm, x_buf, sems.at[0]),
        pltpu.make_async_copy(dy_hbm, dy_buf, sems.at[1]),
    ]
    for load in loads:
        load.start()
    ids = lax.broadcasted_iota(jnp.int32, (experts, 1), 0).astype(F32)
    earlier = (
        lax.broadcasted_iota(jnp.int32, (own, own), 0)
        < lax.broadcasted_iota(jnp.int32, (own, own), 1)
    )
    earlier = jnp.where(earlier, 1.0, 0.0).astype(BF)
    codes, weights = [], []
    for b in range(blocks):
        part = table[b].astype(F32)
        match = jnp.zeros((experts, own), F32)
        weight = jnp.zeros((experts, own), F32)
        for k in range(top):
            hit = part[k : k + 1, :] == ids
            match = match + jnp.where(hit, 1.0, 0.0)
            weight = weight + jnp.where(hit, part[top + k : top + k + 1, :], 0.0)
        rank = jnp.dot(match.astype(BF), earlier, preferred_element_type=F32)
        codes.append(jnp.where(match > 0.0, rank * blocks + b, -1.0))
        weights.append(weight)
    code = jnp.concatenate(codes, axis=1)
    weight = jnp.concatenate(weights, axis=1)
    _, per_expert, feat = x_out.shape
    slots = lax.broadcasted_iota(jnp.int32, (per_expert, 1), 0).astype(F32)
    lanes = lax.broadcasted_iota(jnp.int32, (per_expert, feat), 1)
    diagonal = lanes == lax.broadcasted_iota(jnp.int32, (per_expert, feat), 0)
    for e in range(experts):
        placed = jnp.where(slots == code[e : e + 1, :], 1.0, 0.0)
        coef = jnp.sum(placed * weight[e : e + 1, :], axis=1, keepdims=True)
        coef = jnp.sum(jnp.where(diagonal, coef, 0.0), axis=0, keepdims=True)
        gates[e] = jnp.broadcast_to(coef, (TILE, feat)).astype(BF)
        onehot[e * per_expert : (e + 1) * per_expert, :] = placed.astype(BF)
    for load, src, out in zip(loads, (x_buf, dy_buf), (x_out, dy_out)):
        load.wait()
        rows = jnp.dot(onehot[...], src[...], preferred_element_type=F32).astype(BF)
        rows = rows.reshape(experts, per_expert, feat)
        out[...] = rows


def compact(table, x, dy, experts, per_expert):
    tokens, feat = x.shape
    rows = experts * per_expert
    out = jax.ShapeDtypeStruct((experts, per_expert, feat), BF)
    return pl.pallas_call(
        functools.partial(compact_kernel, experts),
        in_specs=in_vmem(1) + [IN_HBM] * 2,
        out_shape=(
            out,
            out,
            jax.ShapeDtypeStruct((experts, TILE, feat), BF),
            jax.ShapeDtypeStruct((rows, tokens), BF),
        ),
        scratch_shapes=[
            pltpu.VMEM((tokens, feat), BF),
            pltpu.VMEM((tokens, feat), BF),
            pltpu.SemaphoreType.DMA((2,)),
        ],
        compiler_params=params(),
        cost_estimate=cost(4 * rows * tokens * feat, 4 * tokens * feat + 4 * rows * feat),
        name="compact",
    )(table, x, dy)


def in_vmem(count):
    return [pl.BlockSpec(memory_space=pltpu.VMEM)] * count


SCALAR = pl.BlockSpec(memory_space=pltpu.SMEM)
IN_HBM = pl.BlockSpec(memory_space=pl.ANY)


class Queue:
    def __init__(self, groups, ahead):
        self.groups = groups
        self.started = 0
        self.waited = 0
        self.ahead = ahead

    def wait(self):
        while self.started < min(len(self.groups), self.waited + 1 + self.ahead):
            for start, _ in self.groups[self.started]:
                start()
            self.started += 1
        for _, wait in self.groups[self.waited]:
            wait()
        self.waited += 1


def plain(copy):
    return (copy.start, copy.wait)


def column(row, rows):
    shape = (rows, row.shape[1])
    same = lax.broadcasted_iota(jnp.int32, shape, 1) == lax.broadcasted_iota(jnp.int32, shape, 0)
    return jnp.sum(jnp.where(same, row, 0.0), axis=1, keepdims=True)


def block_copies(refs, sources, me, copies):
    out = []
    for k, places in enumerate(sources):
        found = {}
        for j, place in enumerate(places):
            found.setdefault(place, []).append(j)
        options = [(copies(refs[place], k), devices) for place, devices in found.items()]

        def start(options=options):
            if len(options) == 1:
                options[0][0].start()
                return
            for copy, devices in options:
                pl.when(functools.reduce(jnp.logical_or, [me == j for j in devices]))(copy.start)

        out.append((start, options[0][0].wait))
    return out


def line_copies(refs, sources, me, buffer, sems):
    pieces, total, _ = buffer.shape
    rows = total // len(sources)
    return [
        block_copies(
            refs,
            sources,
            me,
            lambda ref, k, f=f: pltpu.make_async_copy(
                ref.at[pl.ds(f * rows, rows), :],
                buffer.at[f, pl.ds(k * rows, rows), :],
                sems.at[f],
            ),
        )
        for f in range(pieces)
    ]


def weight_copies(weights, buffer, sems, pieces, by_rows):
    size = buffer.shape[0 if by_rows else 1] // pieces
    out = []
    for f in range(pieces):
        here = pl.ds(f * size, size)
        at = (here, slice(None)) if by_rows else (slice(None), here)
        out.append(plain(pltpu.make_async_copy(weights.at[(0, *at)], buffer.at[at], sems.at[f])))
    return out


def up_kernel(count, sources, coef_at, me, *refs):
    x, coefs, refs = refs[:count], refs[count : 2 * count], refs[2 * count :]
    w_gate, w_up, gate_pre, up_proj, coef, rows_out = refs[:6]
    x_buf, coef_buf, gate_buf, up_buf, sems, coef_sem = refs[6:]
    pieces, total, feat = x_buf.shape
    blocks = len(sources)
    rows = total // blocks
    x_loads = line_copies(x, sources, me[0], x_buf, sems.at[0])
    gate_loads = weight_copies(w_gate, gate_buf, sems.at[1], pieces, True)
    up_loads = weight_copies(w_up, up_buf, sems.at[2], pieces, True)
    coef_loads = block_copies(
        coefs,
        sources,
        me[0],
        lambda ref, k: pltpu.make_async_copy(
            ref.at[pl.ds(coef_at, TILE), :], coef_buf.at[k], coef_sem.at[0]
        ),
    )
    queue = Queue(
        [[*x_loads[f], gate_loads[f], up_loads[f]] for f in range(pieces)] + [coef_loads], AHEAD
    )
    stores = []
    for f in range(pieces):
        queue.wait()
        stores.append(pltpu.make_async_copy(x_buf.at[f], rows_out.at[f], sems.at[3, f]))
        stores[-1].start()
        here = slice(f * feat, (f + 1) * feat)
        gate = jnp.dot(x_buf[f], gate_buf[here, :], preferred_element_type=F32)
        proj = jnp.dot(x_buf[f], up_buf[here, :], preferred_element_type=F32)
        if f == 0:
            gate_pre[...] = gate
            up_proj[...] = proj
        else:
            gate_pre[...] += gate
            up_proj[...] += proj
    queue.wait()
    for k in range(blocks):
        values = column(coef_buf[k][:1, :].astype(F32), rows)
        coef[k * rows : (k + 1) * rows, :] = jnp.broadcast_to(values, (rows, 128))
    for store in stores:
        store.wait()


def up(me, sources, x, coefs, coef_at, w_gate, w_up):
    feat = x[0].shape[1]
    _, model, hidden = w_gate.shape
    pieces = model // feat
    blocks = len(sources)
    total = x[0].shape[0] // pieces * blocks
    total -= total % (blocks * TILE)
    out = jax.ShapeDtypeStruct((total, hidden), F32)
    return pl.pallas_call(
        functools.partial(up_kernel, len(x), sources, coef_at),
        in_specs=[SCALAR] + [IN_HBM] * (2 * len(x) + 2),
        out_specs=in_vmem(3) + [IN_HBM],
        out_shape=(
            out,
            out,
            jax.ShapeDtypeStruct((total, 128), F32),
            jax.ShapeDtypeStruct((pieces, total, feat), BF),
        ),
        scratch_shapes=[
            pltpu.VMEM((pieces, total, feat), BF),
            pltpu.VMEM((blocks, TILE, coefs[0].shape[1]), BF),
            pltpu.VMEM((model, hidden), BF),
            pltpu.VMEM((model, hidden), BF),
            pltpu.SemaphoreType.DMA((4, pieces)),
            pltpu.SemaphoreType.DMA((1,)),
        ],
        compiler_params=params(),
        cost_estimate=cost(4 * total * model * hidden, 4 * model * hidden),
        name="up",
    )(me, *x, *coefs, w_gate, w_up)


def back_kernel(count, sources, me, *refs):
    dy, refs = refs[:count], refs[count:]
    w_down, w_gate, w_up, coef, gate_pre, up_proj, grad_gate, grad_up, parts = refs[:9]
    dy_buf, down_buf, gate_buf, up_buf, out_buf, sems, out_sems = refs[9:]
    pieces, total, feat = dy_buf.shape
    blocks = len(sources)
    rows = total // blocks
    dy_loads = line_copies(dy, sources, me[0], dy_buf, sems.at[0])
    down_loads = weight_copies(w_down, down_buf, sems.at[1], pieces, False)
    gate_loads = weight_copies(w_gate, gate_buf, sems.at[2], pieces, True)
    up_loads = weight_copies(w_up, up_buf, sems.at[3], pieces, True)
    queue = Queue(
        [[*dy_loads[f], down_loads[f]] for f in range(pieces)]
        + [[gate_loads[f], up_loads[f]] for f in range(pieces)],
        AHEAD,
    )
    value = None
    for f in range(pieces):
        queue.wait()
        here = slice(f * feat, (f + 1) * feat)
        part = lax.dot_general(dy_buf[f], down_buf[:, here], ROWS_DIMS, preferred_element_type=F32)
        value = part if value is None else value + part
    grad_hidden = coef[:, :1] * value
    pre = gate_pre[...]
    sigma = jax.nn.sigmoid(pre)
    grad_gate[...] = (
        grad_hidden * up_proj[...] * sigma * (1.0 + pre * (1.0 - sigma))
    ).astype(BF)
    grad_up[...] = (grad_hidden * (pre * sigma)).astype(BF)
    stores = []
    for f in range(pieces):
        queue.wait()
        here = slice(f * feat, (f + 1) * feat)
        value = lax.dot_general(
            grad_gate[...], gate_buf[here, :], ROWS_DIMS, preferred_element_type=F32
        )
        value += lax.dot_general(
            grad_up[...], up_buf[here, :], ROWS_DIMS, preferred_element_type=F32
        )
        out_buf[f] = value.astype(BF)
        for k in range(blocks):
            stores.append(
                pltpu.make_async_copy(
                    out_buf.at[f, pl.ds(k * rows, rows), :],
                    parts.at[f * blocks + k],
                    out_sems.at[f],
                )
            )
            stores[-1].start()
    for store in stores:
        store.wait()


def back(me, dy, sources, coef, weights, gate_pre, up_proj):
    feat = dy[0].shape[1]
    _, model, hidden = weights[1].shape
    pieces = model // feat
    blocks = len(sources)
    total = gate_pre.shape[0]
    grads = jax.ShapeDtypeStruct((total, hidden), BF)
    return pl.pallas_call(
        functools.partial(back_kernel, len(dy), sources),
        in_specs=[SCALAR] + [IN_HBM] * (len(dy) + 3) + in_vmem(3),
        out_specs=in_vmem(2) + [IN_HBM],
        out_shape=[
            grads,
            grads,
            jax.ShapeDtypeStruct((pieces * blocks, total // blocks, feat), BF),
        ],
        scratch_shapes=[
            pltpu.VMEM((pieces, total, feat), BF),
            pltpu.VMEM((hidden, model), BF),
            pltpu.VMEM((model, hidden), BF),
            pltpu.VMEM((model, hidden), BF),
            pltpu.VMEM((pieces, total, feat), BF),
            pltpu.SemaphoreType.DMA((4, pieces)),
            pltpu.SemaphoreType.DMA((pieces,)),
        ],
        compiler_params=params(),
        cost_estimate=cost(6 * total * model * hidden, 6 * model * hidden),
        name="back",
    )(me, *dy, *weights, coef, gate_pre, up_proj)


def weights_kernel(count, *refs):
    x, (gates, ups, g_gate, g_up) = refs[:count], refs[count:]
    rows = jnp.concatenate([r[0] for r in x], axis=0)
    g_gate[0] = lax.dot_general(rows, gates[...], FIRST_DIMS, preferred_element_type=F32).astype(BF)
    g_up[0] = lax.dot_general(rows, ups[...], FIRST_DIMS, preferred_element_type=F32).astype(BF)


def weight_grads(x, grad_gate, grad_up):
    pieces, _, feat = x[0].shape
    total, hidden = grad_gate.shape
    g_spec = pl.BlockSpec((total, hidden), lambda f: (0, 0))
    o_spec = pl.BlockSpec((1, feat, hidden), lambda f: (0, f, 0))
    out = jax.ShapeDtypeStruct((1, pieces * feat, hidden), BF)
    return pl.pallas_call(
        functools.partial(weights_kernel, len(x)),
        grid=(pieces,),
        in_specs=[pl.BlockSpec((1,) + v.shape[1:], lambda f: (f, 0, 0)) for v in x]
        + [g_spec, g_spec],
        out_specs=(o_spec, o_spec),
        out_shape=(out, out),
        compiler_params=params("arbitrary"),
        cost_estimate=cost(4 * total * pieces * feat * hidden, 4 * pieces * feat * hidden),
        name="weight_grads",
    )(*x, grad_gate, grad_up)


def scatter_kernel(experts, onehot_hbm, parts, out, onehot, buffer, high, low, sems):
    groups = parts.shape[0] // experts
    rows = parts.shape[1]
    queue = Queue(
        [
            [
                plain(
                    pltpu.make_async_copy(
                        parts.at[pl.ds(e * groups, groups)],
                        buffer.at[pl.ds(e * groups, groups)],
                        sems.at[e],
                    )
                )
            ]
            for e in range(experts)
        ]
        + [[plain(pltpu.make_async_copy(onehot_hbm, onehot, sems.at[experts]))]],
        experts,
    )
    for e in range(experts):
        queue.wait()
        here = slice(e * rows, (e + 1) * rows)
        total = buffer[e * groups].astype(F32)
        for g in range(1, groups):
            total += buffer[e * groups + g].astype(F32)
        high[here, :] = total.astype(BF)
        low[here, :] = (total - high[here, :].astype(F32)).astype(BF)
    queue.wait()
    value = lax.dot_general(onehot[...], high[...], FIRST_DIMS, preferred_element_type=F32)
    value += lax.dot_general(onehot[...], low[...], FIRST_DIMS, preferred_element_type=F32)
    out[...] = value.astype(BF)


def scatter(onehot, parts, experts):
    rows, tokens = onehot.shape
    feat = parts.shape[2]
    return pl.pallas_call(
        functools.partial(scatter_kernel, experts),
        in_specs=[IN_HBM] * 2,
        out_shape=jax.ShapeDtypeStruct((tokens, feat), BF),
        scratch_shapes=[
            pltpu.VMEM(onehot.shape, BF),
            pltpu.VMEM(parts.shape, BF),
            pltpu.VMEM((rows, feat), BF),
            pltpu.VMEM((rows, feat), BF),
            pltpu.SemaphoreType.DMA((experts + 1,)),
        ],
        compiler_params=params(),
        cost_estimate=cost(4 * rows * tokens * feat, 2 * rows * tokens + 4 * tokens * feat),
        name="scatter",
    )(onehot, parts)


def together(*groups):
    flat = lax.optimization_barrier([v for g in groups for v in g])
    out = []
    for g in groups:
        out.append(flat[: len(g)])
        flat = flat[len(g) :]
    return out


def send(value, pairs):
    return lax.ppermute(value, "dp", pairs)


class Gather:
    def __init__(self, value):
        self.right = [value]
        self.left = [value]

    def step(self):
        n = lax.axis_size("dp")
        s = len(self.right)
        right, left = self.right[-1], self.left[-1]
        self.right.append(send(right, [(i, i + 1) for i in range(s - 1, n - 1)]))
        self.left.append(send(left, [(i, i - 1) for i in range(1, n - s + 1)]))

    @property
    def last(self):
        return [self.right[-1], self.left[-1]]

    @last.setter
    def last(self, values):
        self.right[-1], self.left[-1] = values

    def arrays(self):
        return self.right + self.left[1:]

    @staticmethod
    def sources(n):
        def place(me, at):
            return me - at if at <= me else n - 1 + at - me

        return tuple(
            tuple(place(me, block) for me in range(n)) for block in range(n)
        )


def widen(values, fold, blocks):
    if fold == 1:
        return values
    count, rows, feat = values.shape
    values = values.reshape(count // (fold * blocks), fold, blocks, rows, feat)
    values = jnp.transpose(values, (0, 2, 3, 1, 4))
    return values.reshape(count // fold, rows, fold * feat)


def narrow(values, fold, blocks):
    if fold == 1:
        return values
    count, rows, feat = values.shape
    values = values.reshape(count // blocks, blocks, rows, fold, feat // fold)
    values = jnp.transpose(values, (0, 3, 1, 2, 4))
    return values.reshape(count * fold, rows, feat // fold)


def per_device(attn_rows, out_grad, routes, gates, w_gate, w_up, w_down):
    experts = lax.axis_size("expert")
    groups = lax.axis_size("dp")
    own, top = routes.shape
    feat = attn_rows.shape[1]
    capacity = 3 * own // 64
    rows = capacity * experts
    fold = 128 // math.gcd(feat, 128)
    pieces = experts // fold
    me = lax.axis_index("dp").astype(jnp.int32)[None]
    sources = Gather.sources(groups)

    def exchange(values, axes):
        return lax.all_to_all(values, axes, split_axis=0, concat_axis=0, tiled=True)

    table = lax.all_gather(label(routes.T, gates.T, experts), "expert", axis=0)
    x, d, coef, onehot = compact(table, attn_rows, out_grad, experts, rows)

    x = exchange(x, "expert")
    coef = lax.dynamic_index_in_dim(coef, lax.axis_index("expert"), 0, keepdims=False)
    (x,), (d,) = together([x], [d])
    gx = Gather(jnp.concatenate([x.reshape(-1, feat), coef], axis=0))
    gx.step()
    d = exchange(d, "expert")
    gx.last, (d,) = together(gx.last, [d])
    gd = Gather(d.reshape(-1, feat))
    for _ in range(groups - 2):
        gx.step()
        gd.step()
    gx.last, gd.last = together(gx.last, gd.last)
    gd.step()
    xs, dy, coefs, coef_at = gx.arrays(), gd.arrays(), gx.arrays(), experts * rows
    if fold > 1:
        xs, dy = [
            [
                widen(v[:coef_at].reshape(experts, rows, feat), fold, 1).reshape(-1, fold * feat)
                for v in arrays
            ]
            for arrays in (xs, dy)
        ]
        coefs = [v[coef_at:] for v in coefs]
        coef_at = 0
    gate_pre, up_proj, coef, x_rows = up(me, sources, xs, coefs, coef_at, w_gate, w_up)
    grad_gate, grad_up, parts = back(
        me, dy, sources, coef, (w_down, w_gate, w_up), gate_pre, up_proj
    )
    parts = exchange(narrow(parts, fold, groups), ("expert", "dp"))
    g_gate, g_up = weight_grads([x_rows], grad_gate, grad_up)
    return scatter(onehot, parts, experts), g_gate, g_up


def solution(mesh):
    return jax.shard_map(
        per_device,
        mesh=mesh,
        in_specs=(
            P("dp", "expert"),
            P("dp", "expert"),
            P(("dp", "expert"), None),
            P(("dp", "expert"), None),
            P("expert", None, "dp"),
            P("expert", None, "dp"),
            P("expert", "dp", None),
        ),
        out_specs=(P("dp", "expert"), P("expert", None, "dp"), P("expert", None, "dp")),
        check_vma=False,
    )
```

```python
import functools
import math

import jax
import jax.numpy as jnp
from jax import lax
from jax.experimental import pallas as pl
from jax.experimental.pallas import tpu as pltpu
from jax.sharding import PartitionSpec as P

BF = jnp.bfloat16
F32 = jnp.float32
TILE = 16
AHEAD = 8
ROWS_DIMS = (((1,), (1,)), ((), ()))
FIRST_DIMS = (((0,), (0,)), ((), ()))


def params(*semantics, limit=58):
    return pltpu.CompilerParams(
        vmem_limit_bytes=limit * 1024 * 1024, dimension_semantics=semantics or None
    )


def cost(flops, moved):
    return pl.CostEstimate(flops=int(flops), bytes_accessed=int(moved), transcendentals=0)


def label(routes, gates, experts):
    top = routes.shape[0]
    named = jnp.pad(jnp.minimum(routes, experts).astype(F32), ((0, top), (0, 0)))
    return (named + jnp.pad(gates.astype(F32), ((top, 0), (0, 0)))).astype(BF)


def compact_kernel(
    experts, first, second, table, x_hbm, dy_hbm, early, late, gates, onehot, x_buf, dy_buf, sems
):
    blocks, labels, own = table.shape
    top = labels // 2
    feat = x_hbm.shape[1]
    loads = [
        pltpu.make_async_copy(x_hbm, x_buf, sems.at[0]),
        pltpu.make_async_copy(dy_hbm, dy_buf, sems.at[1]),
    ]
    for load in loads:
        load.start()
    ids = lax.broadcasted_iota(jnp.int32, (experts, 1), 0).astype(F32)
    earlier = (
        lax.broadcasted_iota(jnp.int32, (own, own), 0)
        < lax.broadcasted_iota(jnp.int32, (own, own), 1)
    )
    earlier = jnp.where(earlier, 1.0, 0.0).astype(BF)
    codes, weights = [], []
    for b in range(blocks):
        part = table[b].astype(F32)
        match = jnp.zeros((experts, own), F32)
        weight = jnp.zeros((experts, own), F32)
        for k in range(top):
            hit = part[k : k + 1, :] == ids
            match = match + jnp.where(hit, 1.0, 0.0)
            weight = weight + jnp.where(hit, part[top + k : top + k + 1, :], 0.0)
        rank = jnp.dot(match.astype(BF), earlier, preferred_element_type=F32)
        codes.append(jnp.where(match > 0.0, rank * blocks + b, -1.0))
        weights.append(weight)
    code = jnp.concatenate(codes, axis=1)
    weight = jnp.concatenate(weights, axis=1)
    per_expert = first + second
    slots = lax.broadcasted_iota(jnp.int32, (per_expert, 1), 0).astype(F32)
    lanes = lax.broadcasted_iota(jnp.int32, (per_expert, feat), 1)
    diagonal = lanes == lax.broadcasted_iota(jnp.int32, (per_expert, feat), 0)
    for e in range(experts):
        placed = jnp.where(slots == code[e : e + 1, :], 1.0, 0.0)
        coef = jnp.sum(placed * weight[e : e + 1, :], axis=1, keepdims=True)
        coef = jnp.sum(jnp.where(diagonal, coef, 0.0), axis=0, keepdims=True)
        gates[e] = jnp.broadcast_to(coef, (TILE, feat)).astype(BF)
        onehot[e * per_expert : (e + 1) * per_expert, :] = placed.astype(BF)
    for k, (load, src) in enumerate(zip(loads, (x_buf, dy_buf))):
        load.wait()
        rows = jnp.dot(onehot[...], src[...], preferred_element_type=F32).astype(BF)
        rows = rows.reshape(experts, per_expert, feat)
        early[:, k * first : (k + 1) * first] = rows[:, :first]
        late[:, k * second : (k + 1) * second] = rows[:, first:]


def compact(table, x, dy, experts, first, second):
    tokens, feat = x.shape
    rows = experts * (first + second)
    return pl.pallas_call(
        functools.partial(compact_kernel, experts, first, second),
        in_specs=in_vmem(1) + [IN_HBM] * 2,
        out_shape=(
            jax.ShapeDtypeStruct((experts, 2 * first, feat), BF),
            jax.ShapeDtypeStruct((experts, 2 * second, feat), BF),
            jax.ShapeDtypeStruct((experts, TILE, feat), BF),
            jax.ShapeDtypeStruct((rows, tokens), BF),
        ),
        scratch_shapes=[
            pltpu.VMEM((tokens, feat), BF),
            pltpu.VMEM((tokens, feat), BF),
            pltpu.SemaphoreType.DMA((2,)),
        ],
        compiler_params=params(),
        cost_estimate=cost(4 * rows * tokens * feat, 4 * tokens * feat + 4 * rows * feat),
        name="compact",
    )(table, x, dy)


def in_vmem(count):
    return [pl.BlockSpec(memory_space=pltpu.VMEM)] * count


SCALAR = pl.BlockSpec(memory_space=pltpu.SMEM)
IN_HBM = pl.BlockSpec(memory_space=pl.ANY)


def column(row, rows):
    shape = (rows, row.shape[1])
    same = lax.broadcasted_iota(jnp.int32, shape, 1) == lax.broadcasted_iota(jnp.int32, shape, 0)
    return jnp.sum(jnp.where(same, row, 0.0), axis=1, keepdims=True)


class Queue:
    def __init__(self, groups, ahead):
        self.groups = groups
        self.started = 0
        self.waited = 0
        self.ahead = ahead

    def wait(self):
        while self.started < min(len(self.groups), self.waited + 1 + self.ahead):
            for start, _ in self.groups[self.started]:
                start()
            self.started += 1
        for _, wait in self.groups[self.waited]:
            wait()
        self.waited += 1


def plain(copy):
    return (copy.start, copy.wait)


def column(row, rows):
    shape = (rows, row.shape[1])
    same = lax.broadcasted_iota(jnp.int32, shape, 1) == lax.broadcasted_iota(jnp.int32, shape, 0)
    return jnp.sum(jnp.where(same, row, 0.0), axis=1, keepdims=True)


def block_copies(refs, choices, end, copies):
    out = []
    for k, choice in enumerate(choices):
        copy = copies(refs[choice[0]], k)
        if len(choice) == 1:
            out.append(plain(copy))
            continue
        other = copies(refs[choice[1]], k)

        def start(copy=copy, other=other):
            pl.when(end == 0)(copy.start)
            pl.when(end != 0)(other.start)

        out.append((start, copy.wait))
    return out


def block_copies(refs, sources, me, copies):
    out = []
    for k, places in enumerate(sources):
        found = {}
        for j, place in enumerate(places):
            found.setdefault(place, []).append(j)
        options = [(copies(refs[place], k), devices) for place, devices in found.items()]

        def start(options=options):
            if len(options) == 1:
                options[0][0].start()
                return
            for copy, devices in options:
                pl.when(functools.reduce(jnp.logical_or, [me == j for j in devices]))(copy.start)

        out.append((start, options[0][0].wait))
    return out


def weight_copies(weights, buffer, sems, pieces, by_rows):
    size = buffer.shape[0 if by_rows else 1] // pieces
    out = []
    for f in range(pieces):
        here = pl.ds(f * size, size)
        at = (here, slice(None)) if by_rows else (slice(None), here)
        out.append(plain(pltpu.make_async_copy(weights.at[(0, *at)], buffer.at[at], sems.at[f])))
    return out


def expert_kernel(counts, sources, coef_sources, start, coef_at, me, *refs):
    blocks = len(sources)
    arrays, refs = refs[: counts[0]], refs[counts[0] :]
    coefs, refs = refs[: counts[1]], refs[counts[1] :]
    w_down, w_gate, w_up, rows_out, grad_gate, grad_up = refs[:6]
    parts, refs = refs[6 : 6 + blocks], refs[6 + blocks :]
    x_buf, dy_buf, coef_buf, down_buf, gate_buf, up_buf, gate_pre, up_proj, out_buf = refs[:-3]
    sems, coef_sem, out_sems = refs[-3:]
    pieces, total, feat = x_buf.shape
    rows = total // blocks

    def load(buffer, second, sem):
        return [
            block_copies(
                arrays,
                sources,
                me[0],
                lambda ref, k, f=f: pltpu.make_async_copy(
                    ref.at[pl.ds((2 * f + second) * rows, rows), :],
                    buffer.at[f, pl.ds(k * rows, rows), :],
                    sem.at[f],
                ),
            )
            for f in range(pieces)
        ]

    coef_loads = block_copies(
        coefs,
        coef_sources,
        me[0],
        lambda ref, k: pltpu.make_async_copy(
            ref.at[pl.ds(coef_at, TILE), :], coef_buf.at[k], coef_sem.at[0]
        ),
    )
    x_loads = load(x_buf, 0, sems.at[0])
    dy_loads = load(dy_buf, 1, sems.at[1])
    down_loads = weight_copies(w_down, down_buf, sems.at[2], pieces, False)
    gate_loads = weight_copies(w_gate, gate_buf, sems.at[3], pieces, True)
    up_loads = weight_copies(w_up, up_buf, sems.at[4], pieces, True)
    queue = Queue(
        [[*dy_loads[f], down_loads[f]] for f in range(pieces)]
        + [coef_loads]
        + [[*x_loads[f], gate_loads[f], up_loads[f]] for f in range(pieces)],
        AHEAD,
    )
    value = None
    for f in range(pieces):
        queue.wait()
        here = slice(f * feat, (f + 1) * feat)
        part = lax.dot_general(dy_buf[f], down_buf[:, here], ROWS_DIMS, preferred_element_type=F32)
        value = part if value is None else value + part
    queue.wait()
    coef = [column(coef_buf[k][:1, :].astype(F32), start + rows)[start:] for k in range(blocks)]
    grad_hidden = jnp.concatenate(coef, axis=0) * value
    stores = []
    for f in range(pieces):
        queue.wait()
        stores.append(pltpu.make_async_copy(x_buf.at[f], rows_out.at[f], out_sems.at[0, f]))
        stores[-1].start()
        here = slice(f * feat, (f + 1) * feat)
        gate = jnp.dot(x_buf[f], gate_buf[here, :], preferred_element_type=F32)
        proj = jnp.dot(x_buf[f], up_buf[here, :], preferred_element_type=F32)
        if f == 0:
            gate_pre[...] = gate
            up_proj[...] = proj
        else:
            gate_pre[...] += gate
            up_proj[...] += proj
    pre = gate_pre[...]
    sigma = jax.nn.sigmoid(pre)
    grad_gate[...] = (
        grad_hidden * up_proj[...] * sigma * (1.0 + pre * (1.0 - sigma))
    ).astype(BF)
    grad_up[...] = (grad_hidden * (pre * sigma)).astype(BF)
    for f in range(pieces):
        here = slice(f * feat, (f + 1) * feat)
        value = lax.dot_general(
            grad_gate[...], gate_buf[here, :], ROWS_DIMS, preferred_element_type=F32
        )
        value += lax.dot_general(
            grad_up[...], up_buf[here, :], ROWS_DIMS, preferred_element_type=F32
        )
        out_buf[f] = value.astype(BF)
        for k in range(blocks):
            stores.append(
                pltpu.make_async_copy(
                    out_buf.at[f, pl.ds(k * rows, rows), :],
                    parts[k].at[f],
                    out_sems.at[1, f],
                )
            )
            stores[-1].start()
    for store in stores:
        store.wait()


def expert_pass(me, sources, arrays, coef_sources, coefs, coef_at, weights, start, rows):
    feat = arrays[0].shape[1]
    _, model, hidden = weights[1].shape
    pieces = model // feat
    blocks = len(sources)
    total = rows * blocks
    grads = jax.ShapeDtypeStruct((total, hidden), BF)
    big = (pieces, total, feat)
    results = pl.pallas_call(
        functools.partial(
            expert_kernel, (len(arrays), len(coefs)), sources, coef_sources, start, coef_at
        ),
        in_specs=[SCALAR] + [IN_HBM] * (len(arrays) + len(coefs) + 3),
        out_specs=[IN_HBM] + in_vmem(2) + [IN_HBM] * blocks,
        out_shape=[
            jax.ShapeDtypeStruct(big, BF),
            grads,
            grads,
        ]
        + [jax.ShapeDtypeStruct((pieces, rows, feat), BF)] * blocks,
        scratch_shapes=[
            pltpu.VMEM(big, BF),
            pltpu.VMEM(big, BF),
            pltpu.VMEM((blocks, TILE, coefs[0].shape[1]), BF),
            pltpu.VMEM((hidden, model), BF),
            pltpu.VMEM((model, hidden), BF),
            pltpu.VMEM((model, hidden), BF),
            pltpu.VMEM((total, hidden), F32),
            pltpu.VMEM((total, hidden), F32),
            pltpu.VMEM(big, BF),
            pltpu.SemaphoreType.DMA((5, pieces)),
            pltpu.SemaphoreType.DMA((1,)),
            pltpu.SemaphoreType.DMA((2, pieces)),
        ],
        compiler_params=params(),
        cost_estimate=cost(10 * total * model * hidden, 6 * model * hidden),
        name="expert",
    )(me, *arrays, *coefs, *weights)
    return results[0], results[1:3], results[3:]


def weights_kernel(count, *refs):
    x, gates, ups = refs[:count], refs[count : 2 * count], refs[2 * count : 3 * count]
    g_gate, g_up = refs[3 * count :]
    rows = jnp.concatenate([r[0] for r in x], axis=0)
    for grads, out in ((gates, g_gate), (ups, g_up)):
        values = jnp.concatenate([r[...] for r in grads], axis=0)
        out[0] = lax.dot_general(
            rows, values, FIRST_DIMS, preferred_element_type=F32
        ).astype(BF)


def weight_grads(x, gates, ups):
    pieces, _, feat = x[0].shape
    hidden = gates[0].shape[1]
    total = sum(v.shape[1] for v in x)
    g_specs = [pl.BlockSpec(v.shape, lambda f: (0, 0)) for v in gates]
    o_spec = pl.BlockSpec((1, feat, hidden), lambda f: (0, f, 0))
    out = jax.ShapeDtypeStruct((1, pieces * feat, hidden), BF)
    return pl.pallas_call(
        functools.partial(weights_kernel, len(x)),
        grid=(pieces,),
        in_specs=[pl.BlockSpec((1,) + v.shape[1:], lambda f: (f, 0, 0)) for v in x]
        + g_specs * 2,
        out_specs=(o_spec, o_spec),
        out_shape=(out, out),
        compiler_params=params("arbitrary"),
        cost_estimate=cost(4 * total * pieces * feat * hidden, 4 * pieces * feat * hidden),
        name="weight_grads",
    )(*x, *gates, *ups)


def scatter_kernel(onehot, rows, out):
    rows = rows[...].reshape(onehot.shape[0], out.shape[1])
    value = lax.dot_general(onehot[...], rows, FIRST_DIMS, preferred_element_type=F32)
    out[...] = value.astype(BF)


def scatter(onehot, values):
    rows, tokens = onehot.shape
    feat = values.shape[2]
    return pl.pallas_call(
        scatter_kernel,
        out_shape=jax.ShapeDtypeStruct((tokens, feat), BF),
        compiler_params=params(limit=16),
        cost_estimate=cost(2 * rows * tokens * feat, 2 * rows * tokens + 4 * tokens * feat),
        name="scatter",
    )(onehot, values)


def together(*groups):
    flat = lax.optimization_barrier([v for g in groups for v in g])
    out = []
    for g in groups:
        out.append(flat[: len(g)])
        flat = flat[len(g) :]
    return out


FOUR = 4
TWO_ON = [(i, (i + 2) % FOUR) for i in range(FOUR)]
PAIRS = [(i, i ^ 1) for i in range(FOUR)]
MIDDLE = [(1, 2), (2, 1)]
OUTWARD = [(1, 0), (2, 3)]
INWARD = [(0, 1), (3, 2)]


def send(value, pairs):
    return lax.ppermute(value, "dp", pairs)


def shift(n, k):
    return [(i, (i + k) % n) for i in range(n)]


def origin(n, block, me):
    return me ^ (0, 2, 1, 3)[block] if n == FOUR else (me - block) % n


class Steps:
    def __init__(self, value):
        self.right = [value]
        self.left = [value]

    def step(self):
        n = lax.axis_size("dp")
        s = len(self.right)
        right, left = self.right[-1], self.left[-1]
        self.right.append(send(right, [(i, i + 1) for i in range(s - 1, n - 1)]))
        self.left.append(send(left, [(i, i - 1) for i in range(1, n - s + 1)]))

    @property
    def last(self):
        return [self.right[-1], self.left[-1]]

    @last.setter
    def last(self, values):
        self.right[-1], self.left[-1] = values

    @property
    def got(self):
        return self.right + self.left[1:]

    @staticmethod
    def sources(n):
        def place(me, at):
            return me - at if at <= me else n - 1 + at - me

        return tuple(tuple(place(j, origin(n, k, j)) for j in range(n)) for k in range(n))


class Gather:
    def __init__(self, value):
        self.got = [value]

    def middle(self):
        if lax.axis_size("dp") == FOUR:
            self.got.append(send(self.got[0], MIDDLE))

    def first(self):
        own, n = self.got[0], lax.axis_size("dp")
        if n == FOUR:
            self.got += [send(own, TWO_ON), send(own, PAIRS)]
        else:
            self.got += [send(own, shift(n, k)) for k in range(1, n)]

    def second(self):
        if lax.axis_size("dp") == FOUR:
            self.got.append(send(self.got[2], OUTWARD))

    @staticmethod
    def sources(n):
        if n == FOUR:
            return ((0,) * n, (2,) * n, (3,) * n, (4, 1, 1, 4))
        return tuple((k,) * n for k in range(n))


def add(*values):
    total = values[0].astype(F32)
    for v in values[1:]:
        total = total + v.astype(F32)
    return total.astype(BF)


class Sum:
    def __init__(self, parts):
        self.parts = parts
        self.got = []

    def first(self):
        n = len(self.parts)
        if n == FOUR:
            self.got = [send(self.parts[3], INWARD), send(self.parts[3], MIDDLE)]
        else:
            self.got = [send(self.parts[k], shift(n, n - k)) for k in range(1, n)]

    def second(self):
        if len(self.parts) == FOUR:
            inward, middle = self.got
            two_on = send(add(self.parts[1], inward), TWO_ON)
            self.got = [two_on, send(self.parts[2], PAIRS), middle]

    def result(self):
        return add(self.parts[0], *self.got)


def widen(values, fold):
    pieces, rows, feat = values.shape
    values = values.reshape(pieces // fold, fold, rows, feat)
    values = jnp.swapaxes(values, 1, 2) if fold > 1 else values
    return values.reshape(pieces // fold * rows, fold * feat)


def narrow(values, fold):
    if fold == 1:
        return values
    pieces, rows, feat = values.shape
    values = values.reshape(pieces, rows, fold, feat // fold)
    return jnp.swapaxes(values, 1, 2).reshape(pieces * fold, rows, feat // fold)


def per_device(attn_rows, out_grad, routes, gates, w_gate, w_up, w_down):
    experts = lax.axis_size("expert")
    groups = lax.axis_size("dp")
    own, top = routes.shape
    feat = attn_rows.shape[1]
    capacity = 3 * own // 64
    late = capacity // 3
    first, second = (capacity - late) * experts, late * experts
    rows = first + second
    fold = 128 // math.gcd(feat, 128)
    pieces = experts // fold
    here = lax.axis_index("dp").astype(jnp.int32)
    me = here[None]
    weights = (w_down, w_gate, w_up)

    def exchange(values):
        return lax.all_to_all(values, "expert", split_axis=0, concat_axis=0, tiled=True)

    table = lax.all_gather(label(routes.T, gates.T, experts), "expert", axis=0)
    early, late, coef, onehot = compact(table, attn_rows, out_grad, experts, first, second)
    early = exchange(early)
    coef = lax.dynamic_index_in_dim(coef, lax.axis_index("expert"), 0, keepdims=False)
    (early, coef), (late,) = together([early, coef], [late])
    one = Steps(jnp.concatenate([early.reshape(-1, feat), coef], axis=0))
    one.step()
    late = exchange(late)
    one.last, (late,) = together(one.last, [late])
    for _ in range(groups - 3):
        one.step()
    one.last, (late,) = together(one.last, [late])
    two = Gather(late.reshape(-1, feat))
    one.step()
    two.middle()
    one.last, two.got = together(one.last, two.got)
    two.first()
    coef_at = 2 * experts * first
    coefs = one.got if fold == 1 else [v[coef_at:] for v in one.got]
    coef_sources = Steps.sources(groups)

    def run(sources, arrays, start, count):
        if fold > 1:
            size = 2 * experts * count
            arrays = [
                widen(v[:size].reshape(experts, 2 * count, feat), fold) for v in arrays
            ]
        at = coef_at if fold == 1 else 0
        x_rows, grads, parts = expert_pass(
            me, sources, arrays, coef_sources, coefs, at, weights, start, count
        )
        return x_rows, grads, [narrow(v, fold) for v in parts]

    xs1, grads1, parts1 = run(coef_sources, one.got, 0, first)
    two.got, parts1 = together(two.got, parts1)
    two.second()
    back1 = Sum(parts1)
    back1.first()
    two.got, back1.got = together(two.got, back1.got)
    back1.second()
    xs2, grads2, parts2 = run(Gather.sources(groups), two.got, first, second)
    back1.got, parts2 = together(back1.got, parts2)
    back2 = Sum(parts2)
    back2.first()
    g_gate, g_up = weight_grads([xs1, xs2], *[list(pair) for pair in zip(grads1, grads2)])
    back2.second()
    total = jnp.concatenate([back1.result(), back2.result()], axis=1)
    return scatter(onehot, exchange(total)), g_gate, g_up


def solution(mesh):
    return jax.shard_map(
        per_device,
        mesh=mesh,
        in_specs=(
            P("dp", "expert"),
            P("dp", "expert"),
            P(("dp", "expert"), None),
            P(("dp", "expert"), None),
            P("expert", None, "dp"),
            P("expert", None, "dp"),
            P("expert", "dp", None),
        ),
        out_specs=(P("dp", "expert"), P("expert", None, "dp"), P("expert", None, "dp")),
        check_vma=False,
    )
```

```python
import functools
import math

import jax
import jax.numpy as jnp
from jax import lax
from jax.experimental import pallas as pl
from jax.experimental.pallas import tpu as pltpu
from jax.sharding import PartitionSpec as P

BF = jnp.bfloat16
F32 = jnp.float32
TILE = 16
AHEAD = 8
ROWS_DIMS = (((1,), (1,)), ((), ()))
FIRST_DIMS = (((0,), (0,)), ((), ()))


def params(*semantics, limit=58):
    return pltpu.CompilerParams(
        vmem_limit_bytes=limit * 1024 * 1024, dimension_semantics=semantics or None
    )


def cost(flops, moved):
    return pl.CostEstimate(flops=int(flops), bytes_accessed=int(moved), transcendentals=0)


def label(routes, gates, experts):
    top = routes.shape[0]
    named = jnp.pad(jnp.minimum(routes, experts).astype(F32), ((0, top), (0, 0)))
    return (named + jnp.pad(gates.astype(F32), ((top, 0), (0, 0)))).astype(BF)


def compact_kernel(
    experts, first, second, table, x_hbm, dy_hbm, early, late, gates, onehot, x_buf, dy_buf, sems
):
    blocks, labels, own = table.shape
    top = labels // 2
    feat = x_hbm.shape[1]
    loads = [
        pltpu.make_async_copy(x_hbm, x_buf, sems.at[0]),
        pltpu.make_async_copy(dy_hbm, dy_buf, sems.at[1]),
    ]
    for load in loads:
        load.start()
    ids = lax.broadcasted_iota(jnp.int32, (experts, 1), 0).astype(F32)
    earlier = (
        lax.broadcasted_iota(jnp.int32, (own, own), 0)
        < lax.broadcasted_iota(jnp.int32, (own, own), 1)
    )
    earlier = jnp.where(earlier, 1.0, 0.0).astype(BF)
    codes, weights = [], []
    for b in range(blocks):
        part = table[b].astype(F32)
        match = jnp.zeros((experts, own), F32)
        weight = jnp.zeros((experts, own), F32)
        for k in range(top):
            hit = part[k : k + 1, :] == ids
            match = match + jnp.where(hit, 1.0, 0.0)
            weight = weight + jnp.where(hit, part[top + k : top + k + 1, :], 0.0)
        rank = jnp.dot(match.astype(BF), earlier, preferred_element_type=F32)
        codes.append(jnp.where(match > 0.0, rank * blocks + b, -1.0))
        weights.append(weight)
    code = jnp.concatenate(codes, axis=1)
    weight = jnp.concatenate(weights, axis=1)
    per_expert = first + second
    slots = lax.broadcasted_iota(jnp.int32, (per_expert, 1), 0).astype(F32)
    lanes = lax.broadcasted_iota(jnp.int32, (per_expert, feat), 1)
    diagonal = lanes == lax.broadcasted_iota(jnp.int32, (per_expert, feat), 0)
    for e in range(experts):
        placed = jnp.where(slots == code[e : e + 1, :], 1.0, 0.0)
        coef = jnp.sum(placed * weight[e : e + 1, :], axis=1, keepdims=True)
        coef = jnp.sum(jnp.where(diagonal, coef, 0.0), axis=0, keepdims=True)
        gates[e] = jnp.broadcast_to(coef, (TILE, feat)).astype(BF)
        onehot[e * per_expert : (e + 1) * per_expert, :] = placed.astype(BF)
    for k, (load, src) in enumerate(zip(loads, (x_buf, dy_buf))):
        load.wait()
        rows = jnp.dot(onehot[...], src[...], preferred_element_type=F32).astype(BF)
        rows = rows.reshape(experts, per_expert, feat)
        early[:, k * first : (k + 1) * first] = rows[:, :first]
        late[:, k * second : (k + 1) * second] = rows[:, first:]


def compact(table, x, dy, experts, first, second):
    tokens, feat = x.shape
    rows = experts * (first + second)
    return pl.pallas_call(
        functools.partial(compact_kernel, experts, first, second),
        in_specs=in_vmem(1) + [IN_HBM] * 2,
        out_shape=(
            jax.ShapeDtypeStruct((experts, 2 * first, feat), BF),
            jax.ShapeDtypeStruct((experts, 2 * second, feat), BF),
            jax.ShapeDtypeStruct((experts, TILE, feat), BF),
            jax.ShapeDtypeStruct((rows, tokens), BF),
        ),
        scratch_shapes=[
            pltpu.VMEM((tokens, feat), BF),
            pltpu.VMEM((tokens, feat), BF),
            pltpu.SemaphoreType.DMA((2,)),
        ],
        compiler_params=params(),
        cost_estimate=cost(4 * rows * tokens * feat, 4 * tokens * feat + 4 * rows * feat),
        name="compact",
    )(table, x, dy)


def in_vmem(count):
    return [pl.BlockSpec(memory_space=pltpu.VMEM)] * count


SCALAR = pl.BlockSpec(memory_space=pltpu.SMEM)
IN_HBM = pl.BlockSpec(memory_space=pl.ANY)


def column(row, rows):
    shape = (rows, row.shape[1])
    same = lax.broadcasted_iota(jnp.int32, shape, 1) == lax.broadcasted_iota(jnp.int32, shape, 0)
    return jnp.sum(jnp.where(same, row, 0.0), axis=1, keepdims=True)


class Queue:
    def __init__(self, groups, ahead):
        self.groups = groups
        self.started = 0
        self.waited = 0
        self.ahead = ahead

    def wait(self):
        while self.started < min(len(self.groups), self.waited + 1 + self.ahead):
            for start, _ in self.groups[self.started]:
                start()
            self.started += 1
        for _, wait in self.groups[self.waited]:
            wait()
        self.waited += 1


def plain(copy):
    return (copy.start, copy.wait)


def column(row, rows):
    shape = (rows, row.shape[1])
    same = lax.broadcasted_iota(jnp.int32, shape, 1) == lax.broadcasted_iota(jnp.int32, shape, 0)
    return jnp.sum(jnp.where(same, row, 0.0), axis=1, keepdims=True)


def block_copies(refs, choices, end, copies):
    out = []
    for k, choice in enumerate(choices):
        copy = copies(refs[choice[0]], k)
        if len(choice) == 1:
            out.append(plain(copy))
            continue
        other = copies(refs[choice[1]], k)

        def start(copy=copy, other=other):
            pl.when(end == 0)(copy.start)
            pl.when(end != 0)(other.start)

        out.append((start, copy.wait))
    return out


def block_copies(refs, sources, me, copies):
    out = []
    for k, places in enumerate(sources):
        found = {}
        for j, place in enumerate(places):
            found.setdefault(place, []).append(j)
        options = [(copies(refs[place], k), devices) for place, devices in found.items()]

        def start(options=options):
            if len(options) == 1:
                options[0][0].start()
                return
            for copy, devices in options:
                pl.when(functools.reduce(jnp.logical_or, [me == j for j in devices]))(copy.start)

        out.append((start, options[0][0].wait))
    return out


def weight_copies(weights, buffer, sems, pieces, by_rows):
    size = buffer.shape[0 if by_rows else 1] // pieces
    out = []
    for f in range(pieces):
        here = pl.ds(f * size, size)
        at = (here, slice(None)) if by_rows else (slice(None), here)
        out.append(plain(pltpu.make_async_copy(weights.at[(0, *at)], buffer.at[at], sems.at[f])))
    return out


def split_refs(counts, refs):
    n, apart = counts[0], counts[2]
    if apart:
        return (refs[:n], refs[n : 2 * n]), (1, 0), refs[2 * n :]
    return (refs[:n], refs[:n]), (2, 1), refs[n:]


def expert_kernel(counts, sources, coef_sources, start, coef_at, me, *refs):
    blocks = len(sources)
    (x, dy), (stride, shift), refs = split_refs(counts, refs)
    coefs, refs = refs[: counts[1]], refs[counts[1] :]
    w_down, w_gate, w_up, rows_out, grad_gate, grad_up = refs[:6]
    parts, refs = refs[6 : 6 + blocks], refs[6 + blocks :]
    x_buf, dy_buf, coef_buf, down_buf, gate_buf, up_buf, gate_pre, up_proj, out_buf = refs[:-3]
    sems, coef_sem, out_sems = refs[-3:]
    pieces, total, feat = x_buf.shape
    rows = total // blocks

    def load(arrays, buffer, shift, sem):
        return [
            block_copies(
                arrays,
                sources,
                me[0],
                lambda ref, k, f=f: pltpu.make_async_copy(
                    ref.at[pl.ds((stride * f + shift) * rows, rows), :],
                    buffer.at[f, pl.ds(k * rows, rows), :],
                    sem.at[f],
                ),
            )
            for f in range(pieces)
        ]

    coef_loads = block_copies(
        coefs,
        coef_sources,
        me[0],
        lambda ref, k: pltpu.make_async_copy(
            ref.at[pl.ds(coef_at, TILE), :], coef_buf.at[k], coef_sem.at[0]
        ),
    )
    x_loads = load(x, x_buf, 0, sems.at[0])
    dy_loads = load(dy, dy_buf, shift, sems.at[1])
    down_loads = weight_copies(w_down, down_buf, sems.at[2], pieces, False)
    gate_loads = weight_copies(w_gate, gate_buf, sems.at[3], pieces, True)
    up_loads = weight_copies(w_up, up_buf, sems.at[4], pieces, True)
    queue = Queue(
        [[*dy_loads[f], down_loads[f]] for f in range(pieces)]
        + [coef_loads]
        + [[*x_loads[f], gate_loads[f], up_loads[f]] for f in range(pieces)],
        AHEAD,
    )
    value = None
    for f in range(pieces):
        queue.wait()
        here = slice(f * feat, (f + 1) * feat)
        part = lax.dot_general(dy_buf[f], down_buf[:, here], ROWS_DIMS, preferred_element_type=F32)
        value = part if value is None else value + part
    queue.wait()
    coef = [column(coef_buf[k][:1, :].astype(F32), start + rows)[start:] for k in range(blocks)]
    grad_hidden = jnp.concatenate(coef, axis=0) * value
    stores = []
    for f in range(pieces):
        queue.wait()
        stores.append(pltpu.make_async_copy(x_buf.at[f], rows_out.at[f], out_sems.at[0, f]))
        stores[-1].start()
        here = slice(f * feat, (f + 1) * feat)
        gate = jnp.dot(x_buf[f], gate_buf[here, :], preferred_element_type=F32)
        proj = jnp.dot(x_buf[f], up_buf[here, :], preferred_element_type=F32)
        if f == 0:
            gate_pre[...] = gate
            up_proj[...] = proj
        else:
            gate_pre[...] += gate
            up_proj[...] += proj
    pre = gate_pre[...]
    sigma = jax.nn.sigmoid(pre)
    grad_gate[...] = (
        grad_hidden * up_proj[...] * sigma * (1.0 + pre * (1.0 - sigma))
    ).astype(BF)
    grad_up[...] = (grad_hidden * (pre * sigma)).astype(BF)
    for f in range(pieces):
        here = slice(f * feat, (f + 1) * feat)
        value = lax.dot_general(
            grad_gate[...], gate_buf[here, :], ROWS_DIMS, preferred_element_type=F32
        )
        value += lax.dot_general(
            grad_up[...], up_buf[here, :], ROWS_DIMS, preferred_element_type=F32
        )
        out_buf[f] = value.astype(BF)
        for k in range(blocks):
            stores.append(
                pltpu.make_async_copy(
                    out_buf.at[f, pl.ds(k * rows, rows), :],
                    parts[k].at[f],
                    out_sems.at[1, f],
                )
            )
            stores[-1].start()
    for store in stores:
        store.wait()


def expert_pass(me, sources, arrays, coef_sources, coefs, coef_at, weights, start, rows):
    feat = arrays[0].shape[1]
    _, model, hidden = weights[1].shape
    pieces = model // feat
    blocks = len(sources)
    apart = len(arrays) > len(coefs) + 1
    count = len(arrays) // 2 if apart else len(arrays)
    total = rows * blocks
    grads = jax.ShapeDtypeStruct((total, hidden), BF)
    big = (pieces, total, feat)
    results = pl.pallas_call(
        functools.partial(
            expert_kernel, (count, len(coefs), apart), sources, coef_sources, start, coef_at
        ),
        in_specs=[SCALAR] + [IN_HBM] * (len(arrays) + len(coefs) + 3),
        out_specs=[IN_HBM] + in_vmem(2) + [IN_HBM] * blocks,
        out_shape=[
            jax.ShapeDtypeStruct(big, BF),
            grads,
            grads,
        ]
        + [jax.ShapeDtypeStruct((pieces, rows, feat), BF)] * blocks,
        scratch_shapes=[
            pltpu.VMEM(big, BF),
            pltpu.VMEM(big, BF),
            pltpu.VMEM((blocks, TILE, coefs[0].shape[1]), BF),
            pltpu.VMEM((hidden, model), BF),
            pltpu.VMEM((model, hidden), BF),
            pltpu.VMEM((model, hidden), BF),
            pltpu.VMEM((total, hidden), F32),
            pltpu.VMEM((total, hidden), F32),
            pltpu.VMEM(big, BF),
            pltpu.SemaphoreType.DMA((5, pieces)),
            pltpu.SemaphoreType.DMA((1,)),
            pltpu.SemaphoreType.DMA((2, pieces)),
        ],
        compiler_params=params(),
        cost_estimate=cost(10 * total * model * hidden, 6 * model * hidden),
        name="expert",
    )(me, *arrays, *coefs, *weights)
    return results[0], results[1:3], results[3:]


def weights_kernel(count, *refs):
    x, gates, ups = refs[:count], refs[count : 2 * count], refs[2 * count : 3 * count]
    g_gate, g_up = refs[3 * count :]
    rows = jnp.concatenate([r[0] for r in x], axis=0)
    for grads, out in ((gates, g_gate), (ups, g_up)):
        values = jnp.concatenate([r[...] for r in grads], axis=0)
        out[0] = lax.dot_general(
            rows, values, FIRST_DIMS, preferred_element_type=F32
        ).astype(BF)


def weight_grads(x, gates, ups):
    pieces, _, feat = x[0].shape
    hidden = gates[0].shape[1]
    total = sum(v.shape[1] for v in x)
    g_specs = [pl.BlockSpec(v.shape, lambda f: (0, 0)) for v in gates]
    o_spec = pl.BlockSpec((1, feat, hidden), lambda f: (0, f, 0))
    out = jax.ShapeDtypeStruct((1, pieces * feat, hidden), BF)
    return pl.pallas_call(
        functools.partial(weights_kernel, len(x)),
        grid=(pieces,),
        in_specs=[pl.BlockSpec((1,) + v.shape[1:], lambda f: (f, 0, 0)) for v in x]
        + g_specs * 2,
        out_specs=(o_spec, o_spec),
        out_shape=(out, out),
        compiler_params=params("arbitrary"),
        cost_estimate=cost(4 * total * pieces * feat * hidden, 4 * pieces * feat * hidden),
        name="weight_grads",
    )(*x, *gates, *ups)


def scatter_kernel(onehot, rows, out):
    rows = rows[...].reshape(onehot.shape[0], out.shape[1])
    value = lax.dot_general(onehot[...], rows, FIRST_DIMS, preferred_element_type=F32)
    out[...] = value.astype(BF)


def scatter(onehot, values):
    rows, tokens = onehot.shape
    feat = values.shape[2]
    return pl.pallas_call(
        scatter_kernel,
        out_shape=jax.ShapeDtypeStruct((tokens, feat), BF),
        compiler_params=params(limit=16),
        cost_estimate=cost(2 * rows * tokens * feat, 2 * rows * tokens + 4 * tokens * feat),
        name="scatter",
    )(onehot, values)


def together(*groups):
    flat = lax.optimization_barrier([v for g in groups for v in g])
    out = []
    for g in groups:
        out.append(flat[: len(g)])
        flat = flat[len(g) :]
    return out


FOUR = 4
TWO_ON = [(i, (i + 2) % FOUR) for i in range(FOUR)]
PAIRS = [(i, i ^ 1) for i in range(FOUR)]
MIDDLE = [(1, 2), (2, 1)]
OUTWARD = [(1, 0), (2, 3)]
INWARD = [(0, 1), (3, 2)]


def send(value, pairs):
    return lax.ppermute(value, "dp", pairs)


def shift(n, k):
    return [(i, (i + k) % n) for i in range(n)]


def origin(n, block, me):
    return me ^ (0, 2, 1, 3)[block] if n == FOUR else (me - block) % n


class Steps:
    def __init__(self, value):
        self.right = [value]
        self.left = [value]

    def step(self):
        n = lax.axis_size("dp")
        s = len(self.right)
        right, left = self.right[-1], self.left[-1]
        self.right.append(send(right, [(i, i + 1) for i in range(s - 1, n - 1)]))
        self.left.append(send(left, [(i, i - 1) for i in range(1, n - s + 1)]))

    @property
    def last(self):
        return [self.right[-1], self.left[-1]]

    @last.setter
    def last(self, values):
        self.right[-1], self.left[-1] = values

    @property
    def got(self):
        return self.right + self.left[1:]

    @staticmethod
    def sources(n):
        def place(me, at):
            return me - at if at <= me else n - 1 + at - me

        return tuple(tuple(place(j, origin(n, k, j)) for j in range(n)) for k in range(n))


class Gather:
    def __init__(self, value):
        self.got = [value]

    def middle(self):
        if lax.axis_size("dp") == FOUR:
            self.got.append(send(self.got[0], MIDDLE))

    def first(self):
        own, n = self.got[0], lax.axis_size("dp")
        if n == FOUR:
            self.got += [send(own, TWO_ON), send(own, PAIRS)]
        else:
            self.got += [send(own, shift(n, k)) for k in range(1, n)]

    def second(self):
        if lax.axis_size("dp") == FOUR:
            self.got.append(send(self.got[2], OUTWARD))

    @staticmethod
    def sources(n):
        if n == FOUR:
            return ((0,) * n, (2,) * n, (3,) * n, (4, 1, 1, 4))
        return tuple((k,) * n for k in range(n))


def add(*values):
    total = values[0].astype(F32)
    for v in values[1:]:
        total = total + v.astype(F32)
    return total.astype(BF)


class Sum:
    def __init__(self, parts):
        self.parts = parts
        self.got = []

    def first(self):
        n = len(self.parts)
        if n == FOUR:
            self.got = [send(self.parts[3], INWARD), send(self.parts[3], MIDDLE)]
        else:
            self.got = [send(self.parts[k], shift(n, n - k)) for k in range(1, n)]

    def second(self):
        if len(self.parts) == FOUR:
            inward, middle = self.got
            two_on = send(add(self.parts[1], inward), TWO_ON)
            self.got = [two_on, send(self.parts[2], PAIRS), middle]

    def result(self):
        return add(self.parts[0], *self.got)


def widen(values, fold):
    pieces, rows, feat = values.shape
    values = values.reshape(pieces // fold, fold, rows, feat)
    values = jnp.swapaxes(values, 1, 2) if fold > 1 else values
    return values.reshape(pieces // fold * rows, fold * feat)


def narrow(values, fold):
    if fold == 1:
        return values
    pieces, rows, feat = values.shape
    values = values.reshape(pieces, rows, fold, feat // fold)
    return jnp.swapaxes(values, 1, 2).reshape(pieces * fold, rows, feat // fold)


def per_device(attn_rows, out_grad, routes, gates, w_gate, w_up, w_down):
    experts = lax.axis_size("expert")
    groups = lax.axis_size("dp")
    own, top = routes.shape
    feat = attn_rows.shape[1]
    capacity = 3 * own // 64
    late = capacity // 3
    first, second = (capacity - late) * experts, late * experts
    rows = first + second
    fold = 128 // math.gcd(feat, 128)
    pieces = experts // fold
    here = lax.axis_index("dp").astype(jnp.int32)
    me = here[None]
    weights = (w_down, w_gate, w_up)

    def exchange(values):
        return lax.all_to_all(values, "expert", split_axis=0, concat_axis=0, tiled=True)

    table = lax.all_gather(label(routes.T, gates.T, experts), "expert", axis=0)
    early, late, coef, onehot = compact(table, attn_rows, out_grad, experts, first, second)
    early = exchange(early)
    coef = lax.dynamic_index_in_dim(coef, lax.axis_index("expert"), 0, keepdims=False)
    (early, coef), (late,) = together([early, coef], [late])
    x = Steps(early[:, :first].reshape(-1, feat))
    dy = Steps(jnp.concatenate([early[:, first:].reshape(-1, feat), coef], axis=0))
    x.step()
    dy.step()
    late = exchange(late)
    x.last, (late,) = together(x.last, [late])
    for _ in range(groups - 3):
        x.step()
        dy.step()
    x.step()
    dy.last, (late,) = together(dy.last, [late])
    two = Gather(late.reshape(-1, feat))
    dy.step()
    two.middle()
    x.last, dy.last, two.got = together(x.last, dy.last, two.got)
    two.first()
    coef_at = experts * first
    coefs = dy.got if fold == 1 else [v[coef_at:] for v in dy.got]
    coef_sources = Steps.sources(groups)

    def run(sources, arrays, start, count, parts_in):
        if fold > 1:
            size = experts * count * parts_in
            arrays = [
                widen(v[:size].reshape(experts, parts_in * count, feat), fold) for v in arrays
            ]
        at = coef_at if fold == 1 else 0
        x_rows, grads, parts = expert_pass(
            me, sources, arrays, coef_sources, coefs, at, weights, start, count
        )
        return x_rows, grads, [narrow(v, fold) for v in parts]

    xs1, grads1, parts1 = run(coef_sources, x.got + dy.got, 0, first, 1)
    two.got, parts1 = together(two.got, parts1)
    two.second()
    back1 = Sum(parts1)
    back1.first()
    two.got, back1.got[:1] = together(two.got, back1.got[:1])
    back1.second()
    xs2, grads2, parts2 = run(Gather.sources(groups), two.got, first, second, 2)
    back1.got, parts2 = together(back1.got, parts2)
    back2 = Sum(parts2)
    back2.first()
    g_gate, g_up = weight_grads([xs1, xs2], *[list(pair) for pair in zip(grads1, grads2)])
    back2.second()
    total = jnp.concatenate([back1.result(), back2.result()], axis=1)
    return scatter(onehot, exchange(total)), g_gate, g_up


def solution(mesh):
    return jax.shard_map(
        per_device,
        mesh=mesh,
        in_specs=(
            P("dp", "expert"),
            P("dp", "expert"),
            P(("dp", "expert"), None),
            P(("dp", "expert"), None),
            P("expert", None, "dp"),
            P("expert", None, "dp"),
            P("expert", "dp", None),
        ),
        out_specs=(P("dp", "expert"), P("expert", None, "dp"), P("expert", None, "dp")),
        check_vma=False,
    )
```

```python
import functools
import math

import jax
import jax.numpy as jnp
from jax import lax
from jax.experimental import pallas as pl
from jax.experimental.pallas import tpu as pltpu
from jax.sharding import PartitionSpec as P

BF = jnp.bfloat16
F32 = jnp.float32
TILE = 16
AHEAD = 8
ROWS_DIMS = (((1,), (1,)), ((), ()))
FIRST_DIMS = (((0,), (0,)), ((), ()))


def params(*semantics, limit=58):
    return pltpu.CompilerParams(
        vmem_limit_bytes=limit * 1024 * 1024, dimension_semantics=semantics or None
    )


def cost(flops, moved):
    return pl.CostEstimate(flops=int(flops), bytes_accessed=int(moved), transcendentals=0)


def label(routes, gates, experts):
    top = routes.shape[0]
    named = jnp.pad(jnp.minimum(routes, experts).astype(F32), ((0, top), (0, 0)))
    return (named + jnp.pad(gates.astype(F32), ((top, 0), (0, 0)))).astype(BF)


def compact_kernel(
    experts, first, second, table, x_hbm, dy_hbm, early, late, gates, onehot, x_buf, dy_buf, sems
):
    blocks, labels, own = table.shape
    top = labels // 2
    feat = x_hbm.shape[1]
    loads = [
        pltpu.make_async_copy(x_hbm, x_buf, sems.at[0]),
        pltpu.make_async_copy(dy_hbm, dy_buf, sems.at[1]),
    ]
    for load in loads:
        load.start()
    ids = lax.broadcasted_iota(jnp.int32, (experts, 1), 0).astype(F32)
    earlier = (
        lax.broadcasted_iota(jnp.int32, (own, own), 0)
        < lax.broadcasted_iota(jnp.int32, (own, own), 1)
    )
    earlier = jnp.where(earlier, 1.0, 0.0).astype(BF)
    codes, weights = [], []
    for b in range(blocks):
        part = table[b].astype(F32)
        match = jnp.zeros((experts, own), F32)
        weight = jnp.zeros((experts, own), F32)
        for k in range(top):
            hit = part[k : k + 1, :] == ids
            match = match + jnp.where(hit, 1.0, 0.0)
            weight = weight + jnp.where(hit, part[top + k : top + k + 1, :], 0.0)
        rank = jnp.dot(match.astype(BF), earlier, preferred_element_type=F32)
        codes.append(jnp.where(match > 0.0, rank * blocks + b, -1.0))
        weights.append(weight)
    code = jnp.concatenate(codes, axis=1)
    weight = jnp.concatenate(weights, axis=1)
    per_expert = first + second
    slots = lax.broadcasted_iota(jnp.int32, (per_expert, 1), 0).astype(F32)
    lanes = lax.broadcasted_iota(jnp.int32, (per_expert, feat), 1)
    diagonal = lanes == lax.broadcasted_iota(jnp.int32, (per_expert, feat), 0)
    for e in range(experts):
        placed = jnp.where(slots == code[e : e + 1, :], 1.0, 0.0)
        coef = jnp.sum(placed * weight[e : e + 1, :], axis=1, keepdims=True)
        coef = jnp.sum(jnp.where(diagonal, coef, 0.0), axis=0, keepdims=True)
        gates[e] = jnp.broadcast_to(coef, (TILE, feat)).astype(BF)
        onehot[e * per_expert : (e + 1) * per_expert, :] = placed.astype(BF)
    for k, (load, src) in enumerate(zip(loads, (x_buf, dy_buf))):
        load.wait()
        rows = jnp.dot(onehot[...], src[...], preferred_element_type=F32).astype(BF)
        rows = rows.reshape(experts, per_expert, feat)
        early[:, k * first : (k + 1) * first] = rows[:, :first]
        late[:, k * second : (k + 1) * second] = rows[:, first:]


def compact(table, x, dy, experts, first, second):
    tokens, feat = x.shape
    rows = experts * (first + second)
    return pl.pallas_call(
        functools.partial(compact_kernel, experts, first, second),
        in_specs=in_vmem(1) + [IN_HBM] * 2,
        out_shape=(
            jax.ShapeDtypeStruct((experts, 2 * first, feat), BF),
            jax.ShapeDtypeStruct((experts, 2 * second, feat), BF),
            jax.ShapeDtypeStruct((experts, TILE, feat), BF),
            jax.ShapeDtypeStruct((rows, tokens), BF),
        ),
        scratch_shapes=[
            pltpu.VMEM((tokens, feat), BF),
            pltpu.VMEM((tokens, feat), BF),
            pltpu.SemaphoreType.DMA((2,)),
        ],
        compiler_params=params(),
        cost_estimate=cost(4 * rows * tokens * feat, 4 * tokens * feat + 4 * rows * feat),
        name="compact",
    )(table, x, dy)


def in_vmem(count):
    return [pl.BlockSpec(memory_space=pltpu.VMEM)] * count


SCALAR = pl.BlockSpec(memory_space=pltpu.SMEM)
IN_HBM = pl.BlockSpec(memory_space=pl.ANY)


def column(row, rows):
    shape = (rows, row.shape[1])
    same = lax.broadcasted_iota(jnp.int32, shape, 1) == lax.broadcasted_iota(jnp.int32, shape, 0)
    return jnp.sum(jnp.where(same, row, 0.0), axis=1, keepdims=True)


class Queue:
    def __init__(self, groups, ahead):
        self.groups = groups
        self.started = 0
        self.waited = 0
        self.ahead = ahead

    def wait(self):
        while self.started < min(len(self.groups), self.waited + 1 + self.ahead):
            for start, _ in self.groups[self.started]:
                start()
            self.started += 1
        for _, wait in self.groups[self.waited]:
            wait()
        self.waited += 1


def plain(copy):
    return (copy.start, copy.wait)


def column(row, rows):
    shape = (rows, row.shape[1])
    same = lax.broadcasted_iota(jnp.int32, shape, 1) == lax.broadcasted_iota(jnp.int32, shape, 0)
    return jnp.sum(jnp.where(same, row, 0.0), axis=1, keepdims=True)


def block_copies(refs, choices, end, copies):
    out = []
    for k, choice in enumerate(choices):
        copy = copies(refs[choice[0]], k)
        if len(choice) == 1:
            out.append(plain(copy))
            continue
        other = copies(refs[choice[1]], k)

        def start(copy=copy, other=other):
            pl.when(end == 0)(copy.start)
            pl.when(end != 0)(other.start)

        out.append((start, copy.wait))
    return out


def block_copies(refs, sources, me, copies):
    out = []
    for k, places in enumerate(sources):
        found = {}
        for j, place in enumerate(places):
            found.setdefault(place, []).append(j)
        options = [(copies(refs[place], k), devices) for place, devices in found.items()]

        def start(options=options):
            if len(options) == 1:
                options[0][0].start()
                return
            for copy, devices in options:
                pl.when(functools.reduce(jnp.logical_or, [me == j for j in devices]))(copy.start)

        out.append((start, options[0][0].wait))
    return out


def weight_copies(weights, buffer, sems, pieces, by_rows):
    size = buffer.shape[0 if by_rows else 1] // pieces
    out = []
    for f in range(pieces):
        here = pl.ds(f * size, size)
        at = (here, slice(None)) if by_rows else (slice(None), here)
        out.append(plain(pltpu.make_async_copy(weights.at[(0, *at)], buffer.at[at], sems.at[f])))
    return out


def split_refs(counts, refs):
    n, apart = counts[0], counts[2]
    if apart:
        return (refs[:n], refs[n : 2 * n]), (1, 0), refs[2 * n :]
    return (refs[:n], refs[:n]), (2, 1), refs[n:]


def expert_kernel(counts, sources, coef_sources, start, coef_at, me, *refs):
    blocks = len(sources)
    refs = refs[counts[3] :]
    (x, dy), (stride, shift), refs = split_refs(counts, refs)
    coefs, refs = refs[: counts[1]], refs[counts[1] :]
    w_down, w_gate, w_up, rows_out, grad_gate, grad_up = refs[:6]
    parts, refs = refs[6 : 6 + blocks], refs[6 + blocks :]
    x_buf, dy_buf, coef_buf, down_buf, gate_buf, up_buf, gate_pre, up_proj, out_buf = refs[:-3]
    sems, coef_sem, out_sems = refs[-3:]
    pieces, total, feat = x_buf.shape
    rows = total // blocks

    def load(arrays, buffer, shift, sem):
        return [
            block_copies(
                arrays,
                sources,
                me[0],
                lambda ref, k, f=f: pltpu.make_async_copy(
                    ref.at[pl.ds((stride * f + shift) * rows, rows), :],
                    buffer.at[f, pl.ds(k * rows, rows), :],
                    sem.at[f],
                ),
            )
            for f in range(pieces)
        ]

    coef_loads = block_copies(
        coefs,
        coef_sources,
        me[0],
        lambda ref, k: pltpu.make_async_copy(
            ref.at[pl.ds(coef_at, TILE), :], coef_buf.at[k], coef_sem.at[0]
        ),
    )
    x_loads = load(x, x_buf, 0, sems.at[0])
    dy_loads = load(dy, dy_buf, shift, sems.at[1])
    down_loads = weight_copies(w_down, down_buf, sems.at[2], pieces, False)
    gate_loads = weight_copies(w_gate, gate_buf, sems.at[3], pieces, True)
    up_loads = weight_copies(w_up, up_buf, sems.at[4], pieces, True)
    queue = Queue(
        [[*dy_loads[f], down_loads[f]] for f in range(pieces)]
        + [coef_loads]
        + [[*x_loads[f], gate_loads[f], up_loads[f]] for f in range(pieces)],
        AHEAD,
    )
    value = None
    for f in range(pieces):
        queue.wait()
        here = slice(f * feat, (f + 1) * feat)
        part = lax.dot_general(dy_buf[f], down_buf[:, here], ROWS_DIMS, preferred_element_type=F32)
        value = part if value is None else value + part
    queue.wait()
    coef = [column(coef_buf[k][:1, :].astype(F32), start + rows)[start:] for k in range(blocks)]
    grad_hidden = jnp.concatenate(coef, axis=0) * value
    stores = []
    for f in range(pieces):
        queue.wait()
        stores.append(pltpu.make_async_copy(x_buf.at[f], rows_out.at[f], out_sems.at[0, f]))
        stores[-1].start()
        here = slice(f * feat, (f + 1) * feat)
        gate = jnp.dot(x_buf[f], gate_buf[here, :], preferred_element_type=F32)
        proj = jnp.dot(x_buf[f], up_buf[here, :], preferred_element_type=F32)
        if f == 0:
            gate_pre[...] = gate
            up_proj[...] = proj
        else:
            gate_pre[...] += gate
            up_proj[...] += proj
    pre = gate_pre[...]
    sigma = jax.nn.sigmoid(pre)
    grad_gate[...] = (
        grad_hidden * up_proj[...] * sigma * (1.0 + pre * (1.0 - sigma))
    ).astype(BF)
    grad_up[...] = (grad_hidden * (pre * sigma)).astype(BF)
    for f in range(pieces):
        here = slice(f * feat, (f + 1) * feat)
        value = lax.dot_general(
            grad_gate[...], gate_buf[here, :], ROWS_DIMS, preferred_element_type=F32
        )
        value += lax.dot_general(
            grad_up[...], up_buf[here, :], ROWS_DIMS, preferred_element_type=F32
        )
        out_buf[f] = value.astype(BF)
        for k in range(blocks):
            stores.append(
                pltpu.make_async_copy(
                    out_buf.at[f, pl.ds(k * rows, rows), :],
                    parts[k].at[f],
                    out_sems.at[1, f],
                )
            )
            stores[-1].start()
    for store in stores:
        store.wait()


def expert_pass(me, sources, arrays, coef_sources, coefs, coef_at, weights, start, rows, after):
    feat = arrays[0].shape[1]
    _, model, hidden = weights[1].shape
    pieces = model // feat
    blocks = len(sources)
    apart = len(arrays) > len(coefs) + 1
    count = len(arrays) // 2 if apart else len(arrays)
    total = rows * blocks
    grads = jax.ShapeDtypeStruct((total, hidden), BF)
    big = (pieces, total, feat)
    results = pl.pallas_call(
        functools.partial(
            expert_kernel, (count, len(coefs), apart, len(after)), sources, coef_sources, start, coef_at
        ),
        in_specs=[SCALAR] + [IN_HBM] * (len(after) + len(arrays) + len(coefs) + 3),
        out_specs=[IN_HBM] + in_vmem(2) + [IN_HBM] * blocks,
        out_shape=[
            jax.ShapeDtypeStruct(big, BF),
            grads,
            grads,
        ]
        + [jax.ShapeDtypeStruct((pieces, rows, feat), BF)] * blocks,
        scratch_shapes=[
            pltpu.VMEM(big, BF),
            pltpu.VMEM(big, BF),
            pltpu.VMEM((blocks, TILE, coefs[0].shape[1]), BF),
            pltpu.VMEM((hidden, model), BF),
            pltpu.VMEM((model, hidden), BF),
            pltpu.VMEM((model, hidden), BF),
            pltpu.VMEM((total, hidden), F32),
            pltpu.VMEM((total, hidden), F32),
            pltpu.VMEM(big, BF),
            pltpu.SemaphoreType.DMA((5, pieces)),
            pltpu.SemaphoreType.DMA((1,)),
            pltpu.SemaphoreType.DMA((2, pieces)),
        ],
        compiler_params=params(),
        cost_estimate=cost(100 * total * model * hidden, 60 * model * hidden),
        name="expert",
    )(me, *after, *arrays, *coefs, *weights)
    return results[0], results[1:3], results[3:]


def weights_kernel(count, *refs):
    x, gates, ups = refs[:count], refs[count : 2 * count], refs[2 * count : 3 * count]
    g_gate, g_up = refs[3 * count :]
    rows = jnp.concatenate([r[0] for r in x], axis=0)
    for grads, out in ((gates, g_gate), (ups, g_up)):
        values = jnp.concatenate([r[...] for r in grads], axis=0)
        out[0] = lax.dot_general(
            rows, values, FIRST_DIMS, preferred_element_type=F32
        ).astype(BF)


def weight_grads(x, gates, ups):
    pieces, _, feat = x[0].shape
    hidden = gates[0].shape[1]
    total = sum(v.shape[1] for v in x)
    g_specs = [pl.BlockSpec(v.shape, lambda f: (0, 0)) for v in gates]
    o_spec = pl.BlockSpec((1, feat, hidden), lambda f: (0, f, 0))
    out = jax.ShapeDtypeStruct((1, pieces * feat, hidden), BF)
    return pl.pallas_call(
        functools.partial(weights_kernel, len(x)),
        grid=(pieces,),
        in_specs=[pl.BlockSpec((1,) + v.shape[1:], lambda f: (f, 0, 0)) for v in x]
        + g_specs * 2,
        out_specs=(o_spec, o_spec),
        out_shape=(out, out),
        compiler_params=params("arbitrary"),
        cost_estimate=cost(4 * total * pieces * feat * hidden, 4 * pieces * feat * hidden),
        name="weight_grads",
    )(*x, *gates, *ups)


def scatter_kernel(onehot, rows, out):
    rows = rows[...].reshape(onehot.shape[0], out.shape[1])
    value = lax.dot_general(onehot[...], rows, FIRST_DIMS, preferred_element_type=F32)
    out[...] = value.astype(BF)


def scatter(onehot, values):
    rows, tokens = onehot.shape
    feat = values.shape[2]
    return pl.pallas_call(
        scatter_kernel,
        out_shape=jax.ShapeDtypeStruct((tokens, feat), BF),
        compiler_params=params(limit=16),
        cost_estimate=cost(2 * rows * tokens * feat, 2 * rows * tokens + 4 * tokens * feat),
        name="scatter",
    )(onehot, values)


def together(*groups):
    flat = lax.optimization_barrier([v for g in groups for v in g])
    out = []
    for g in groups:
        out.append(flat[: len(g)])
        flat = flat[len(g) :]
    return out


FOUR = 4
TWO_ON = [(i, (i + 2) % FOUR) for i in range(FOUR)]
PAIRS = [(i, i ^ 1) for i in range(FOUR)]
MIDDLE = [(1, 2), (2, 1)]
OUTWARD = [(1, 0), (2, 3)]
INWARD = [(0, 1), (3, 2)]


def send(value, pairs):
    return lax.ppermute(value, "dp", pairs)


def shift(n, k):
    return [(i, (i + k) % n) for i in range(n)]


def origin(n, block, me):
    return me ^ (0, 2, 1, 3)[block] if n == FOUR else (me - block) % n


class Steps:
    def __init__(self, value):
        self.right = [value]
        self.left = [value]

    def step(self):
        n = lax.axis_size("dp")
        s = len(self.right)
        right, left = self.right[-1], self.left[-1]
        self.right.append(send(right, [(i, i + 1) for i in range(s - 1, n - 1)]))
        self.left.append(send(left, [(i, i - 1) for i in range(1, n - s + 1)]))

    @property
    def last(self):
        return [self.right[-1], self.left[-1]]

    @last.setter
    def last(self, values):
        self.right[-1], self.left[-1] = values

    @property
    def got(self):
        return self.right + self.left[1:]

    @staticmethod
    def sources(n):
        def place(me, at):
            return me - at if at <= me else n - 1 + at - me

        return tuple(tuple(place(j, origin(n, k, j)) for j in range(n)) for k in range(n))


class Gather:
    def __init__(self, value):
        self.got = [value]

    def middle(self):
        if lax.axis_size("dp") == FOUR:
            self.got.append(send(self.got[0], MIDDLE))

    def first(self):
        own, n = self.got[0], lax.axis_size("dp")
        if n == FOUR:
            self.got += [send(own, TWO_ON), send(own, PAIRS)]
        else:
            self.got += [send(own, shift(n, k)) for k in range(1, n)]

    def second(self):
        if lax.axis_size("dp") == FOUR:
            self.got.append(send(self.got[2], OUTWARD))

    @staticmethod
    def sources(n):
        if n == FOUR:
            return ((0,) * n, (2,) * n, (3,) * n, (4, 1, 1, 4))
        return tuple((k,) * n for k in range(n))


def add(*values):
    total = values[0].astype(F32)
    for v in values[1:]:
        total = total + v.astype(F32)
    return total.astype(BF)


class Sum:
    def __init__(self, parts):
        self.parts = parts
        self.got = []
        self.sent = []

    def first(self, last=None):
        n = len(self.parts)
        if n == FOUR:
            last = self.parts[3] if last is None else last
            self.got = [send(last, INWARD), send(self.parts[3], MIDDLE)]
        else:
            self.got = [send(self.parts[k], shift(n, n - k)) for k in range(1, n)]

    def second(self):
        if len(self.parts) == FOUR:
            inward, middle = self.got
            self.sent = [add(self.parts[1], inward)]
            self.got = [send(self.sent[0], TWO_ON), send(self.parts[2], PAIRS), middle]

    def result(self):
        return add(self.parts[0], *self.got)


def widen(values, fold):
    pieces, rows, feat = values.shape
    values = values.reshape(pieces // fold, fold, rows, feat)
    values = jnp.swapaxes(values, 1, 2) if fold > 1 else values
    return values.reshape(pieces // fold * rows, fold * feat)


def narrow(values, fold):
    if fold == 1:
        return values
    pieces, rows, feat = values.shape
    values = values.reshape(pieces, rows, fold, feat // fold)
    return jnp.swapaxes(values, 1, 2).reshape(pieces * fold, rows, feat // fold)


def per_device(attn_rows, out_grad, routes, gates, w_gate, w_up, w_down):
    experts = lax.axis_size("expert")
    groups = lax.axis_size("dp")
    own, top = routes.shape
    feat = attn_rows.shape[1]
    capacity = 3 * own // 64
    late = capacity // 3
    first, second = (capacity - late) * experts, late * experts
    rows = first + second
    fold = 128 // math.gcd(feat, 128)
    pieces = experts // fold
    here = lax.axis_index("dp").astype(jnp.int32)
    me = here[None]
    weights = (w_down, w_gate, w_up)

    def exchange(values):
        return lax.all_to_all(values, "expert", split_axis=0, concat_axis=0, tiled=True)

    table = lax.all_gather(label(routes.T, gates.T, experts), "expert", axis=0)
    early, late, coef, onehot = compact(table, attn_rows, out_grad, experts, first, second)
    early = exchange(early)
    coef = lax.dynamic_index_in_dim(coef, lax.axis_index("expert"), 0, keepdims=False)
    (early, coef), (late,) = together([early, coef], [late])
    x = Steps(early[:, :first].reshape(-1, feat))
    dy = Steps(jnp.concatenate([early[:, first:].reshape(-1, feat), coef], axis=0))
    x.step()
    dy.step()
    late = exchange(late)
    x.last, (late,) = together(x.last, [late])
    for _ in range(groups - 3):
        x.step()
        dy.step()
    x.step()
    dy.last, (late,) = together(dy.last, [late])
    two = Gather(late.reshape(-1, feat))
    dy.step()
    two.middle()
    x.last, dy.last, two.got = together(x.last, dy.last, two.got)
    two.first()
    coef_at = experts * first
    coefs = dy.got if fold == 1 else [v[coef_at:] for v in dy.got]
    coef_sources = Steps.sources(groups)

    def run(sources, arrays, start, count, parts_in, after=()):
        if fold > 1:
            size = experts * count * parts_in
            arrays = [
                widen(v[:size].reshape(experts, parts_in * count, feat), fold) for v in arrays
            ]
        at = coef_at if fold == 1 else 0
        x_rows, grads, parts = expert_pass(
            me, sources, arrays, coef_sources, coefs, at, weights, start, count, after
        )
        return x_rows, grads, [narrow(v, fold) for v in parts]

    xs1, grads1, parts1 = run(coef_sources, x.got + dy.got, 0, first, 1)
    last1 = parts1[3 % groups]
    two.got, parts1 = together(two.got, parts1)
    two.second()
    back1 = Sum(parts1)
    back1.first(last1)
    back1.second()
    xs2, grads2, parts2 = run(
        Gather.sources(groups), two.got, first, second, 2, back1.sent
    )
    last2 = parts2[3 % groups]
    back1.got, parts2 = together(back1.got, parts2)
    back2 = Sum(parts2)
    back2.first(last2)
    g_gate, g_up = weight_grads([xs1, xs2], *[list(pair) for pair in zip(grads1, grads2)])
    back2.second()
    total = jnp.concatenate([back1.result(), back2.result()], axis=1)
    return scatter(onehot, exchange(total)), g_gate, g_up


def solution(mesh):
    return jax.shard_map(
        per_device,
        mesh=mesh,
        in_specs=(
            P("dp", "expert"),
            P("dp", "expert"),
            P(("dp", "expert"), None),
            P(("dp", "expert"), None),
            P("expert", None, "dp"),
            P("expert", None, "dp"),
            P("expert", "dp", None),
        ),
        out_specs=(P("dp", "expert"), P("expert", None, "dp"), P("expert", None, "dp")),
        check_vma=False,
    )
```

```python
import functools
import math

import jax
import jax.numpy as jnp
from jax import lax
from jax.experimental import pallas as pl
from jax.experimental.pallas import tpu as pltpu
from jax.sharding import PartitionSpec as P

BF = jnp.bfloat16
F32 = jnp.float32
TILE = 16
AHEAD = 8
ROWS_DIMS = (((1,), (1,)), ((), ()))
FIRST_DIMS = (((0,), (0,)), ((), ()))


def params(*semantics, limit=58):
    return pltpu.CompilerParams(
        vmem_limit_bytes=limit * 1024 * 1024, dimension_semantics=semantics or None
    )


def cost(flops, moved):
    return pl.CostEstimate(flops=int(flops), bytes_accessed=int(moved), transcendentals=0)


def label(routes, gates, experts):
    top = routes.shape[0]
    named = jnp.pad(jnp.minimum(routes, experts).astype(F32), ((0, top), (0, 0)))
    return (named + jnp.pad(gates.astype(F32), ((top, 0), (0, 0)))).astype(BF)


def compact_kernel(
    experts, first, second, table, x_hbm, dy_hbm, early, late, gates, onehot, x_buf, dy_buf, sems
):
    blocks, labels, own = table.shape
    top = labels // 2
    feat = x_hbm.shape[1]
    loads = [
        pltpu.make_async_copy(x_hbm, x_buf, sems.at[0]),
        pltpu.make_async_copy(dy_hbm, dy_buf, sems.at[1]),
    ]
    for load in loads:
        load.start()
    ids = lax.broadcasted_iota(jnp.int32, (experts, 1), 0).astype(F32)
    earlier = (
        lax.broadcasted_iota(jnp.int32, (own, own), 0)
        < lax.broadcasted_iota(jnp.int32, (own, own), 1)
    )
    earlier = jnp.where(earlier, 1.0, 0.0).astype(BF)
    codes, weights = [], []
    for b in range(blocks):
        part = table[b].astype(F32)
        match = jnp.zeros((experts, own), F32)
        weight = jnp.zeros((experts, own), F32)
        for k in range(top):
            hit = part[k : k + 1, :] == ids
            match = match + jnp.where(hit, 1.0, 0.0)
            weight = weight + jnp.where(hit, part[top + k : top + k + 1, :], 0.0)
        rank = jnp.dot(match.astype(BF), earlier, preferred_element_type=F32)
        codes.append(jnp.where(match > 0.0, rank * blocks + b, -1.0))
        weights.append(weight)
    code = jnp.concatenate(codes, axis=1)
    weight = jnp.concatenate(weights, axis=1)
    per_expert = first + second
    slots = lax.broadcasted_iota(jnp.int32, (per_expert, 1), 0).astype(F32)
    lanes = lax.broadcasted_iota(jnp.int32, (per_expert, feat), 1)
    diagonal = lanes == lax.broadcasted_iota(jnp.int32, (per_expert, feat), 0)
    for e in range(experts):
        placed = jnp.where(slots == code[e : e + 1, :], 1.0, 0.0)
        coef = jnp.sum(placed * weight[e : e + 1, :], axis=1, keepdims=True)
        coef = jnp.sum(jnp.where(diagonal, coef, 0.0), axis=0, keepdims=True)
        gates[e] = jnp.broadcast_to(coef, (TILE, feat)).astype(BF)
        onehot[e * per_expert : (e + 1) * per_expert, :] = placed.astype(BF)
    for k, (load, src) in enumerate(zip(loads, (x_buf, dy_buf))):
        load.wait()
        rows = jnp.dot(onehot[...], src[...], preferred_element_type=F32).astype(BF)
        rows = rows.reshape(experts, per_expert, feat)
        early[:, k * first : (k + 1) * first] = rows[:, :first]
        late[:, k * second : (k + 1) * second] = rows[:, first:]


def compact(table, x, dy, experts, first, second):
    tokens, feat = x.shape
    rows = experts * (first + second)
    return pl.pallas_call(
        functools.partial(compact_kernel, experts, first, second),
        in_specs=in_vmem(1) + [IN_HBM] * 2,
        out_shape=(
            jax.ShapeDtypeStruct((experts, 2 * first, feat), BF),
            jax.ShapeDtypeStruct((experts, 2 * second, feat), BF),
            jax.ShapeDtypeStruct((experts, TILE, feat), BF),
            jax.ShapeDtypeStruct((rows, tokens), BF),
        ),
        scratch_shapes=[
            pltpu.VMEM((tokens, feat), BF),
            pltpu.VMEM((tokens, feat), BF),
            pltpu.SemaphoreType.DMA((2,)),
        ],
        compiler_params=params(),
        cost_estimate=cost(4 * rows * tokens * feat, 4 * tokens * feat + 4 * rows * feat),
        name="compact",
    )(table, x, dy)


def in_vmem(count):
    return [pl.BlockSpec(memory_space=pltpu.VMEM)] * count


SCALAR = pl.BlockSpec(memory_space=pltpu.SMEM)
IN_HBM = pl.BlockSpec(memory_space=pl.ANY)


def column(row, rows):
    shape = (rows, row.shape[1])
    same = lax.broadcasted_iota(jnp.int32, shape, 1) == lax.broadcasted_iota(jnp.int32, shape, 0)
    return jnp.sum(jnp.where(same, row, 0.0), axis=1, keepdims=True)


class Queue:
    def __init__(self, groups, ahead):
        self.groups = groups
        self.started = 0
        self.waited = 0
        self.ahead = ahead

    def wait(self):
        while self.started < min(len(self.groups), self.waited + 1 + self.ahead):
            for start, _ in self.groups[self.started]:
                start()
            self.started += 1
        for _, wait in self.groups[self.waited]:
            wait()
        self.waited += 1


def plain(copy):
    return (copy.start, copy.wait)


def column(row, rows):
    shape = (rows, row.shape[1])
    same = lax.broadcasted_iota(jnp.int32, shape, 1) == lax.broadcasted_iota(jnp.int32, shape, 0)
    return jnp.sum(jnp.where(same, row, 0.0), axis=1, keepdims=True)


def block_copies(refs, choices, end, copies):
    out = []
    for k, choice in enumerate(choices):
        copy = copies(refs[choice[0]], k)
        if len(choice) == 1:
            out.append(plain(copy))
            continue
        other = copies(refs[choice[1]], k)

        def start(copy=copy, other=other):
            pl.when(end == 0)(copy.start)
            pl.when(end != 0)(other.start)

        out.append((start, copy.wait))
    return out


def block_copies(refs, sources, me, copies):
    out = []
    for k, places in enumerate(sources):
        found = {}
        for j, place in enumerate(places):
            found.setdefault(place, []).append(j)
        options = [(copies(refs[place], k), devices) for place, devices in found.items()]

        def start(options=options):
            if len(options) == 1:
                options[0][0].start()
                return
            for copy, devices in options:
                pl.when(functools.reduce(jnp.logical_or, [me == j for j in devices]))(copy.start)

        out.append((start, options[0][0].wait))
    return out


def weight_copies(weights, buffer, sems, pieces, by_rows):
    size = buffer.shape[0 if by_rows else 1] // pieces
    out = []
    for f in range(pieces):
        here = pl.ds(f * size, size)
        at = (here, slice(None)) if by_rows else (slice(None), here)
        out.append(plain(pltpu.make_async_copy(weights.at[(0, *at)], buffer.at[at], sems.at[f])))
    return out


def split_refs(counts, refs):
    n, apart = counts[0], counts[2]
    if apart:
        return (refs[:n], refs[n : 2 * n]), (1, 0), refs[2 * n :]
    return (refs[:n], refs[:n]), (2, 1), refs[n:]


def expert_kernel(counts, sources, coef_sources, start, coef_at, me, *refs):
    blocks = len(sources)
    refs = refs[counts[3] :]
    (x, dy), (stride, shift), refs = split_refs(counts, refs)
    coefs, refs = refs[: counts[1]], refs[counts[1] :]
    w_down, w_gate, w_up, rows_out, grad_gate, grad_up = refs[:6]
    parts, refs = refs[6 : 6 + blocks], refs[6 + blocks :]
    x_buf, dy_buf, coef_buf, down_buf, gate_buf, up_buf, gate_pre, up_proj, out_buf = refs[:-3]
    sems, coef_sem, out_sems = refs[-3:]
    pieces, total, feat = x_buf.shape
    rows = total // blocks

    def load(arrays, buffer, shift, sem):
        return [
            block_copies(
                arrays,
                sources,
                me[0],
                lambda ref, k, f=f: pltpu.make_async_copy(
                    ref.at[pl.ds((stride * f + shift) * rows, rows), :],
                    buffer.at[f, pl.ds(k * rows, rows), :],
                    sem.at[f],
                ),
            )
            for f in range(pieces)
        ]

    coef_loads = block_copies(
        coefs,
        coef_sources,
        me[0],
        lambda ref, k: pltpu.make_async_copy(
            ref.at[pl.ds(coef_at, TILE), :], coef_buf.at[k], coef_sem.at[0]
        ),
    )
    x_loads = load(x, x_buf, 0, sems.at[0])
    dy_loads = load(dy, dy_buf, shift, sems.at[1])
    down_loads = weight_copies(w_down, down_buf, sems.at[2], pieces, False)
    gate_loads = weight_copies(w_gate, gate_buf, sems.at[3], pieces, True)
    up_loads = weight_copies(w_up, up_buf, sems.at[4], pieces, True)
    queue = Queue(
        [[*dy_loads[f], down_loads[f]] for f in range(pieces)]
        + [coef_loads]
        + [[*x_loads[f], gate_loads[f], up_loads[f]] for f in range(pieces)],
        AHEAD,
    )
    value = None
    for f in range(pieces):
        queue.wait()
        here = slice(f * feat, (f + 1) * feat)
        part = lax.dot_general(dy_buf[f], down_buf[:, here], ROWS_DIMS, preferred_element_type=F32)
        value = part if value is None else value + part
    queue.wait()
    coef = [column(coef_buf[k][:1, :].astype(F32), start + rows)[start:] for k in range(blocks)]
    grad_hidden = jnp.concatenate(coef, axis=0) * value
    stores = []
    for f in range(pieces):
        queue.wait()
        stores.append(pltpu.make_async_copy(x_buf.at[f], rows_out.at[f], out_sems.at[0, f]))
        stores[-1].start()
        here = slice(f * feat, (f + 1) * feat)
        gate = jnp.dot(x_buf[f], gate_buf[here, :], preferred_element_type=F32)
        proj = jnp.dot(x_buf[f], up_buf[here, :], preferred_element_type=F32)
        if f == 0:
            gate_pre[...] = gate
            up_proj[...] = proj
        else:
            gate_pre[...] += gate
            up_proj[...] += proj
    pre = gate_pre[...]
    sigma = jax.nn.sigmoid(pre)
    grad_gate[...] = (
        grad_hidden * up_proj[...] * sigma * (1.0 + pre * (1.0 - sigma))
    ).astype(BF)
    grad_up[...] = (grad_hidden * (pre * sigma)).astype(BF)
    for f in range(pieces):
        here = slice(f * feat, (f + 1) * feat)
        value = lax.dot_general(
            grad_gate[...], gate_buf[here, :], ROWS_DIMS, preferred_element_type=F32
        )
        value += lax.dot_general(
            grad_up[...], up_buf[here, :], ROWS_DIMS, preferred_element_type=F32
        )
        out_buf[f] = value.astype(BF)
        for k in range(blocks):
            stores.append(
                pltpu.make_async_copy(
                    out_buf.at[f, pl.ds(k * rows, rows), :],
                    parts[k].at[f],
                    out_sems.at[1, f],
                )
            )
            stores[-1].start()
    for store in stores:
        store.wait()


def expert_pass(me, sources, arrays, coef_sources, coefs, coef_at, weights, start, rows, after):
    feat = arrays[0].shape[1]
    _, model, hidden = weights[1].shape
    pieces = model // feat
    blocks = len(sources)
    apart = len(arrays) > len(coefs) + 1
    count = len(arrays) // 2 if apart else len(arrays)
    total = rows * blocks
    grads = jax.ShapeDtypeStruct((total, hidden), BF)
    big = (pieces, total, feat)
    results = pl.pallas_call(
        functools.partial(
            expert_kernel, (count, len(coefs), apart, len(after)), sources, coef_sources, start, coef_at
        ),
        in_specs=[SCALAR] + [IN_HBM] * (len(after) + len(arrays) + len(coefs) + 3),
        out_specs=[IN_HBM] + in_vmem(2) + [IN_HBM] * blocks,
        out_shape=[
            jax.ShapeDtypeStruct(big, BF),
            grads,
            grads,
        ]
        + [jax.ShapeDtypeStruct((pieces, rows, feat), BF)] * blocks,
        scratch_shapes=[
            pltpu.VMEM(big, BF),
            pltpu.VMEM(big, BF),
            pltpu.VMEM((blocks, TILE, coefs[0].shape[1]), BF),
            pltpu.VMEM((hidden, model), BF),
            pltpu.VMEM((model, hidden), BF),
            pltpu.VMEM((model, hidden), BF),
            pltpu.VMEM((total, hidden), F32),
            pltpu.VMEM((total, hidden), F32),
            pltpu.VMEM(big, BF),
            pltpu.SemaphoreType.DMA((5, pieces)),
            pltpu.SemaphoreType.DMA((1,)),
            pltpu.SemaphoreType.DMA((2, pieces)),
        ],
        compiler_params=params(),
        cost_estimate=cost(100 * total * model * hidden, 60 * model * hidden),
        name="expert",
    )(me, *after, *arrays, *coefs, *weights)
    return results[0], results[1:3], results[3:]


def weights_kernel(count, *refs):
    x, gates, ups = refs[:count], refs[count : 2 * count], refs[2 * count : 3 * count]
    g_gate, g_up = refs[3 * count :]
    rows = jnp.concatenate([r[0] for r in x], axis=0)
    for grads, out in ((gates, g_gate), (ups, g_up)):
        values = jnp.concatenate([r[...] for r in grads], axis=0)
        out[0] = lax.dot_general(
            rows, values, FIRST_DIMS, preferred_element_type=F32
        ).astype(BF)


def weight_grads(x, gates, ups):
    pieces, _, feat = x[0].shape
    hidden = gates[0].shape[1]
    total = sum(v.shape[1] for v in x)
    g_specs = [pl.BlockSpec(v.shape, lambda f: (0, 0)) for v in gates]
    o_spec = pl.BlockSpec((1, feat, hidden), lambda f: (0, f, 0))
    out = jax.ShapeDtypeStruct((1, pieces * feat, hidden), BF)
    return pl.pallas_call(
        functools.partial(weights_kernel, len(x)),
        grid=(pieces,),
        in_specs=[pl.BlockSpec((1,) + v.shape[1:], lambda f: (f, 0, 0)) for v in x]
        + g_specs * 2,
        out_specs=(o_spec, o_spec),
        out_shape=(out, out),
        compiler_params=params("arbitrary"),
        cost_estimate=cost(4 * total * pieces * feat * hidden, 4 * pieces * feat * hidden),
        name="weight_grads",
    )(*x, *gates, *ups)


def scatter_kernel(onehot, rows, out):
    rows = rows[...].reshape(onehot.shape[0], out.shape[1])
    value = lax.dot_general(onehot[...], rows, FIRST_DIMS, preferred_element_type=F32)
    out[...] = value.astype(BF)


def scatter(onehot, values):
    rows, tokens = onehot.shape
    feat = values.shape[2]
    return pl.pallas_call(
        scatter_kernel,
        out_shape=jax.ShapeDtypeStruct((tokens, feat), BF),
        compiler_params=params(limit=16),
        cost_estimate=cost(2 * rows * tokens * feat, 2 * rows * tokens + 4 * tokens * feat),
        name="scatter",
    )(onehot, values)


def together(*groups):
    flat = lax.optimization_barrier([v for g in groups for v in g])
    out = []
    for g in groups:
        out.append(flat[: len(g)])
        flat = flat[len(g) :]
    return out


FOUR = 4
TWO_ON = [(i, (i + 2) % FOUR) for i in range(FOUR)]
PAIRS = [(i, i ^ 1) for i in range(FOUR)]
MIDDLE = [(1, 2), (2, 1)]
OUTWARD = [(1, 0), (2, 3)]
INWARD = [(0, 1), (3, 2)]


def send(value, pairs):
    return lax.ppermute(value, "dp", pairs)


def shift(n, k):
    return [(i, (i + k) % n) for i in range(n)]


def origin(n, block, me):
    return me ^ (0, 2, 1, 3)[block] if n == FOUR else (me - block) % n


class Steps:
    def __init__(self, value):
        self.right = [value]
        self.left = [value]

    def step(self):
        n = lax.axis_size("dp")
        s = len(self.right)
        right, left = self.right[-1], self.left[-1]
        self.right.append(send(right, [(i, i + 1) for i in range(s - 1, n - 1)]))
        self.left.append(send(left, [(i, i - 1) for i in range(1, n - s + 1)]))

    @property
    def last(self):
        return [self.right[-1], self.left[-1]]

    @last.setter
    def last(self, values):
        self.right[-1], self.left[-1] = values

    @property
    def got(self):
        return self.right + self.left[1:]

    @staticmethod
    def sources(n):
        def place(me, at):
            return me - at if at <= me else n - 1 + at - me

        return tuple(tuple(place(j, origin(n, k, j)) for j in range(n)) for k in range(n))


class Gather:
    def __init__(self, value):
        self.got = [value]

    def middle(self):
        if lax.axis_size("dp") == FOUR:
            self.got.append(send(self.got[0], MIDDLE))

    def first(self):
        own, n = self.got[0], lax.axis_size("dp")
        if n == FOUR:
            self.got += [send(own, TWO_ON), send(own, PAIRS)]
        else:
            self.got += [send(own, shift(n, k)) for k in range(1, n)]

    def second(self):
        if lax.axis_size("dp") == FOUR:
            self.got.append(send(self.got[2], OUTWARD))

    @staticmethod
    def sources(n):
        if n == FOUR:
            return ((0,) * n, (2,) * n, (3,) * n, (4, 1, 1, 4))
        return tuple((k,) * n for k in range(n))


def add(*values):
    total = values[0].astype(F32)
    for v in values[1:]:
        total = total + v.astype(F32)
    return total.astype(BF)


class Sum:
    def __init__(self, parts):
        self.parts = parts
        self.got = []
        self.sent = []

    def first(self, last=None):
        n = len(self.parts)
        if n == FOUR:
            last = self.parts[3] if last is None else last
            self.got = [send(last, INWARD), send(self.parts[3], MIDDLE)]
        else:
            self.got = [send(self.parts[k], shift(n, n - k)) for k in range(1, n)]

    def second(self):
        if len(self.parts) == FOUR:
            inward, middle = self.got
            self.sent = [add(self.parts[1], inward)]
            self.got = [send(self.sent[0], TWO_ON), send(self.parts[2], PAIRS), middle]

    def result(self):
        return add(self.parts[0], *self.got)


def widen(values, fold):
    pieces, rows, feat = values.shape
    values = values.reshape(pieces // fold, fold, rows, feat)
    values = jnp.swapaxes(values, 1, 2) if fold > 1 else values
    return values.reshape(pieces // fold * rows, fold * feat)


def narrow(values, fold):
    if fold == 1:
        return values
    pieces, rows, feat = values.shape
    values = values.reshape(pieces, rows, fold, feat // fold)
    return jnp.swapaxes(values, 1, 2).reshape(pieces * fold, rows, feat // fold)


def per_device(attn_rows, out_grad, routes, gates, w_gate, w_up, w_down):
    experts = lax.axis_size("expert")
    groups = lax.axis_size("dp")
    own, top = routes.shape
    feat = attn_rows.shape[1]
    capacity = 3 * own // 64
    late = capacity // 3
    first, second = (capacity - late) * experts, late * experts
    rows = first + second
    fold = 128 // math.gcd(feat, 128)
    pieces = experts // fold
    here = lax.axis_index("dp").astype(jnp.int32)
    me = here[None]
    weights = (w_down, w_gate, w_up)

    def exchange(values):
        return lax.all_to_all(values, "expert", split_axis=0, concat_axis=0, tiled=True)

    table = lax.all_gather(label(routes.T, gates.T, experts), "expert", axis=0)
    early, late, coef, onehot = compact(table, attn_rows, out_grad, experts, first, second)
    early = exchange(early)
    coef = lax.dynamic_index_in_dim(coef, lax.axis_index("expert"), 0, keepdims=False)
    (early, coef), (late,) = together([early, coef], [late])
    x = Steps(early[:, :first].reshape(-1, feat))
    dy = Steps(jnp.concatenate([early[:, first:].reshape(-1, feat), coef], axis=0))
    x.step()
    dy.step()
    late = exchange(late)
    x.last, (late,) = together(x.last, [late])
    for _ in range(groups - 3):
        x.step()
        dy.step()
    x.step()
    dy.last, (late,) = together(dy.last, [late])
    two = Gather(late.reshape(-1, feat))
    dy.step()
    two.middle()
    x.last, dy.last, two.got = together(x.last, dy.last, two.got)
    two.first()
    coef_at = experts * first
    coefs = dy.got if fold == 1 else [v[coef_at:] for v in dy.got]
    coef_sources = Steps.sources(groups)

    def run(sources, arrays, start, count, parts_in, after=()):
        if fold > 1:
            size = experts * count * parts_in
            arrays = [
                widen(v[:size].reshape(experts, parts_in * count, feat), fold) for v in arrays
            ]
        at = coef_at if fold == 1 else 0
        x_rows, grads, parts = expert_pass(
            me, sources, arrays, coef_sources, coefs, at, weights, start, count, after
        )
        return x_rows, grads, [narrow(v, fold) for v in parts]

    xs1, grads1, parts1 = run(coef_sources, x.got + dy.got, 0, first, 1)
    last1 = parts1[3 % groups]
    two.got, parts1 = together(two.got, parts1)
    two.second()
    back1 = Sum(parts1)
    back1.first(last1)
    back1.parts = list(back1.parts)
    two.got, back1.parts[2:3] = together(two.got, back1.parts[2:3])
    back1.second()
    xs2, grads2, parts2 = run(
        Gather.sources(groups), two.got, first, second, 2, back1.sent
    )
    last2 = parts2[3 % groups]
    back1.got, parts2 = together(back1.got, parts2)
    back2 = Sum(parts2)
    back2.first(last2)
    g_gate, g_up = weight_grads([xs1, xs2], *[list(pair) for pair in zip(grads1, grads2)])
    back2.second()
    total = jnp.concatenate([back1.result(), back2.result()], axis=1)
    return scatter(onehot, exchange(total)), g_gate, g_up


def solution(mesh):
    return jax.shard_map(
        per_device,
        mesh=mesh,
        in_specs=(
            P("dp", "expert"),
            P("dp", "expert"),
            P(("dp", "expert"), None),
            P(("dp", "expert"), None),
            P("expert", None, "dp"),
            P("expert", None, "dp"),
            P("expert", "dp", None),
        ),
        out_specs=(P("dp", "expert"), P("expert", None, "dp"), P("expert", None, "dp")),
        check_vma=False,
    )
```

```python
import functools
import math

import jax
import jax.numpy as jnp
from jax import lax
from jax.experimental import pallas as pl
from jax.experimental.pallas import tpu as pltpu
from jax.sharding import PartitionSpec as P

BF = jnp.bfloat16
F32 = jnp.float32
TILE = 16
AHEAD = 8
ROWS_DIMS = (((1,), (1,)), ((), ()))
FIRST_DIMS = (((0,), (0,)), ((), ()))


def params(*semantics, limit=58):
    return pltpu.CompilerParams(
        vmem_limit_bytes=limit * 1024 * 1024, dimension_semantics=semantics or None
    )


def cost(flops, moved):
    return pl.CostEstimate(flops=int(flops), bytes_accessed=int(moved), transcendentals=0)


def label(routes, gates, experts):
    top = routes.shape[0]
    named = jnp.pad(jnp.minimum(routes, experts).astype(F32), ((0, top), (0, 0)))
    return (named + jnp.pad(gates.astype(F32), ((top, 0), (0, 0)))).astype(BF)


def compact_kernel(
    experts, first, second, table, x_hbm, dy_hbm, early, late, gates, onehot, x_buf, dy_buf, sems
):
    blocks, labels, own = table.shape
    top = labels // 2
    feat = x_hbm.shape[1]
    loads = [
        pltpu.make_async_copy(x_hbm, x_buf, sems.at[0]),
        pltpu.make_async_copy(dy_hbm, dy_buf, sems.at[1]),
    ]
    for load in loads:
        load.start()
    ids = lax.broadcasted_iota(jnp.int32, (experts, 1), 0).astype(F32)
    earlier = (
        lax.broadcasted_iota(jnp.int32, (own, own), 0)
        < lax.broadcasted_iota(jnp.int32, (own, own), 1)
    )
    earlier = jnp.where(earlier, 1.0, 0.0).astype(BF)
    codes, weights = [], []
    for b in range(blocks):
        part = table[b].astype(F32)
        match = jnp.zeros((experts, own), F32)
        weight = jnp.zeros((experts, own), F32)
        for k in range(top):
            hit = part[k : k + 1, :] == ids
            match = match + jnp.where(hit, 1.0, 0.0)
            weight = weight + jnp.where(hit, part[top + k : top + k + 1, :], 0.0)
        rank = jnp.dot(match.astype(BF), earlier, preferred_element_type=F32)
        codes.append(jnp.where(match > 0.0, rank * blocks + b, -1.0))
        weights.append(weight)
    code = jnp.concatenate(codes, axis=1)
    weight = jnp.concatenate(weights, axis=1)
    per_expert = first + second
    slots = lax.broadcasted_iota(jnp.int32, (per_expert, 1), 0).astype(F32)
    lanes = lax.broadcasted_iota(jnp.int32, (per_expert, feat), 1)
    diagonal = lanes == lax.broadcasted_iota(jnp.int32, (per_expert, feat), 0)
    for e in range(experts):
        placed = jnp.where(slots == code[e : e + 1, :], 1.0, 0.0)
        coef = jnp.sum(placed * weight[e : e + 1, :], axis=1, keepdims=True)
        coef = jnp.sum(jnp.where(diagonal, coef, 0.0), axis=0, keepdims=True)
        gates[e] = jnp.broadcast_to(coef, (TILE, feat)).astype(BF)
        onehot[e * per_expert : (e + 1) * per_expert, :] = placed.astype(BF)
    for k, (load, src) in enumerate(zip(loads, (x_buf, dy_buf))):
        load.wait()
        rows = jnp.dot(onehot[...], src[...], preferred_element_type=F32).astype(BF)
        rows = rows.reshape(experts, per_expert, feat)
        early[:, k * first : (k + 1) * first] = rows[:, :first]
        late[:, k * second : (k + 1) * second] = rows[:, first:]


def compact(table, x, dy, experts, first, second):
    tokens, feat = x.shape
    rows = experts * (first + second)
    return pl.pallas_call(
        functools.partial(compact_kernel, experts, first, second),
        in_specs=in_vmem(1) + [IN_HBM] * 2,
        out_shape=(
            jax.ShapeDtypeStruct((experts, 2 * first, feat), BF),
            jax.ShapeDtypeStruct((experts, 2 * second, feat), BF),
            jax.ShapeDtypeStruct((experts, TILE, feat), BF),
            jax.ShapeDtypeStruct((rows, tokens), BF),
        ),
        scratch_shapes=[
            pltpu.VMEM((tokens, feat), BF),
            pltpu.VMEM((tokens, feat), BF),
            pltpu.SemaphoreType.DMA((2,)),
        ],
        compiler_params=params(),
        cost_estimate=cost(4 * rows * tokens * feat, 4 * tokens * feat + 4 * rows * feat),
        name="compact",
    )(table, x, dy)


def in_vmem(count):
    return [pl.BlockSpec(memory_space=pltpu.VMEM)] * count


SCALAR = pl.BlockSpec(memory_space=pltpu.SMEM)
IN_HBM = pl.BlockSpec(memory_space=pl.ANY)


def column(row, rows):
    shape = (rows, row.shape[1])
    same = lax.broadcasted_iota(jnp.int32, shape, 1) == lax.broadcasted_iota(jnp.int32, shape, 0)
    return jnp.sum(jnp.where(same, row, 0.0), axis=1, keepdims=True)


class Queue:
    def __init__(self, groups, ahead):
        self.groups = groups
        self.started = 0
        self.waited = 0
        self.ahead = ahead

    def wait(self):
        while self.started < min(len(self.groups), self.waited + 1 + self.ahead):
            for start, _ in self.groups[self.started]:
                start()
            self.started += 1
        for _, wait in self.groups[self.waited]:
            wait()
        self.waited += 1


def plain(copy):
    return (copy.start, copy.wait)


def column(row, rows):
    shape = (rows, row.shape[1])
    same = lax.broadcasted_iota(jnp.int32, shape, 1) == lax.broadcasted_iota(jnp.int32, shape, 0)
    return jnp.sum(jnp.where(same, row, 0.0), axis=1, keepdims=True)


def block_copies(refs, choices, end, copies):
    out = []
    for k, choice in enumerate(choices):
        copy = copies(refs[choice[0]], k)
        if len(choice) == 1:
            out.append(plain(copy))
            continue
        other = copies(refs[choice[1]], k)

        def start(copy=copy, other=other):
            pl.when(end == 0)(copy.start)
            pl.when(end != 0)(other.start)

        out.append((start, copy.wait))
    return out


def block_copies(refs, sources, me, copies):
    out = []
    for k, places in enumerate(sources):
        found = {}
        for j, place in enumerate(places):
            found.setdefault(place, []).append(j)
        options = [(copies(refs[place], k), devices) for place, devices in found.items()]

        def start(options=options):
            if len(options) == 1:
                options[0][0].start()
                return
            for copy, devices in options:
                pl.when(functools.reduce(jnp.logical_or, [me == j for j in devices]))(copy.start)

        out.append((start, options[0][0].wait))
    return out


def weight_copies(weights, buffer, sems, pieces, by_rows):
    size = buffer.shape[0 if by_rows else 1] // pieces
    out = []
    for f in range(pieces):
        here = pl.ds(f * size, size)
        at = (here, slice(None)) if by_rows else (slice(None), here)
        out.append(plain(pltpu.make_async_copy(weights.at[(0, *at)], buffer.at[at], sems.at[f])))
    return out


def split_refs(counts, refs):
    n, apart = counts[0], counts[2]
    if apart:
        return (refs[:n], refs[n : 2 * n]), (1, 0), refs[2 * n :]
    return (refs[:n], refs[:n]), (2, 1), refs[n:]


def expert_kernel(counts, sources, coef_sources, start, coef_at, me, *refs):
    blocks = len(sources)
    refs = refs[counts[3] :]
    (x, dy), (stride, shift), refs = split_refs(counts, refs)
    coefs, refs = refs[: counts[1]], refs[counts[1] :]
    w_down, w_gate, w_up, rows_out, grad_gate, grad_up = refs[:6]
    parts, refs = refs[6 : 6 + blocks], refs[6 + blocks :]
    x_buf, dy_buf, coef_buf, down_buf, both_buf, both_pre, out_buf = refs[:-3]
    sems, coef_sem, out_sems = refs[-3:]
    pieces, total, feat = x_buf.shape
    rows = total // blocks

    def load(arrays, buffer, shift, sem):
        return [
            block_copies(
                arrays,
                sources,
                me[0],
                lambda ref, k, f=f: pltpu.make_async_copy(
                    ref.at[pl.ds((stride * f + shift) * rows, rows), :],
                    buffer.at[f, pl.ds(k * rows, rows), :],
                    sem.at[f],
                ),
            )
            for f in range(pieces)
        ]

    coef_loads = block_copies(
        coefs,
        coef_sources,
        me[0],
        lambda ref, k: pltpu.make_async_copy(
            ref.at[pl.ds(coef_at, TILE), :], coef_buf.at[k], coef_sem.at[0]
        ),
    )
    x_loads = load(x, x_buf, 0, sems.at[0])
    dy_loads = load(dy, dy_buf, shift, sems.at[1])
    down_loads = weight_copies(w_down, down_buf, sems.at[2], pieces, False)
    hidden = down_buf.shape[0]
    gate_loads = weight_copies(
        w_gate, both_buf.at[:, :hidden], sems.at[3], pieces, True
    )
    up_loads = weight_copies(
        w_up, both_buf.at[:, hidden:], sems.at[4], pieces, True
    )
    queue = Queue(
        [[*dy_loads[f], down_loads[f]] for f in range(pieces)]
        + [coef_loads]
        + [[*x_loads[f], gate_loads[f], up_loads[f]] for f in range(pieces)],
        AHEAD,
    )
    value = None
    for f in range(pieces):
        queue.wait()
        here = slice(f * feat, (f + 1) * feat)
        part = lax.dot_general(dy_buf[f], down_buf[:, here], ROWS_DIMS, preferred_element_type=F32)
        value = part if value is None else value + part
    queue.wait()
    coef = [column(coef_buf[k][:1, :].astype(F32), start + rows)[start:] for k in range(blocks)]
    grad_hidden = jnp.concatenate(coef, axis=0) * value
    stores = []
    for f in range(pieces):
        queue.wait()
        stores.append(pltpu.make_async_copy(x_buf.at[f], rows_out.at[f], out_sems.at[0, f]))
        stores[-1].start()
        here = slice(f * feat, (f + 1) * feat)
        both = jnp.dot(x_buf[f], both_buf[here, :], preferred_element_type=F32)
        if f == 0:
            both_pre[...] = both
        else:
            both_pre[...] += both
    pre, proj = both_pre[:, :hidden], both_pre[:, hidden:]
    sigma = jax.nn.sigmoid(pre)
    grad_gate[...] = (
        grad_hidden * proj * sigma * (1.0 + pre * (1.0 - sigma))
    ).astype(BF)
    grad_up[...] = (grad_hidden * (pre * sigma)).astype(BF)
    both_grads = jnp.concatenate([grad_gate[...], grad_up[...]], axis=1)
    for f in range(pieces):
        here = slice(f * feat, (f + 1) * feat)
        value = lax.dot_general(
            both_grads, both_buf[here, :], ROWS_DIMS, preferred_element_type=F32
        )
        out_buf[f] = value.astype(BF)
        for k in range(blocks):
            stores.append(
                pltpu.make_async_copy(
                    out_buf.at[f, pl.ds(k * rows, rows), :],
                    parts[k].at[f],
                    out_sems.at[1, f],
                )
            )
            stores[-1].start()
    for store in stores:
        store.wait()


def expert_pass(me, sources, arrays, coef_sources, coefs, coef_at, weights, start, rows, after):
    feat = arrays[0].shape[1]
    _, model, hidden = weights[1].shape
    pieces = model // feat
    blocks = len(sources)
    apart = len(arrays) > len(coefs) + 1
    count = len(arrays) // 2 if apart else len(arrays)
    total = rows * blocks
    grads = jax.ShapeDtypeStruct((total, hidden), BF)
    big = (pieces, total, feat)
    results = pl.pallas_call(
        functools.partial(
            expert_kernel, (count, len(coefs), apart, len(after)), sources, coef_sources, start, coef_at
        ),
        in_specs=[SCALAR] + [IN_HBM] * (len(after) + len(arrays) + len(coefs) + 3),
        out_specs=[IN_HBM] + in_vmem(2) + [IN_HBM] * blocks,
        out_shape=[
            jax.ShapeDtypeStruct(big, BF),
            grads,
            grads,
        ]
        + [jax.ShapeDtypeStruct((pieces, rows, feat), BF)] * blocks,
        scratch_shapes=[
            pltpu.VMEM(big, BF),
            pltpu.VMEM(big, BF),
            pltpu.VMEM((blocks, TILE, coefs[0].shape[1]), BF),
            pltpu.VMEM((hidden, model), BF),
            pltpu.VMEM((model, 2 * hidden), BF),
            pltpu.VMEM((total, 2 * hidden), F32),
            pltpu.VMEM(big, BF),
            pltpu.SemaphoreType.DMA((5, pieces)),
            pltpu.SemaphoreType.DMA((1,)),
            pltpu.SemaphoreType.DMA((2, pieces)),
        ],
        compiler_params=params(),
        cost_estimate=cost(100 * total * model * hidden, 60 * model * hidden),
        name="expert",
    )(me, *after, *arrays, *coefs, *weights)
    return results[0], results[1:3], results[3:]


def weights_kernel(count, *refs):
    x, gates, ups = refs[:count], refs[count : 2 * count], refs[2 * count : 3 * count]
    g_gate, g_up = refs[3 * count :]
    rows = jnp.concatenate([r[0] for r in x], axis=0)
    for grads, out in ((gates, g_gate), (ups, g_up)):
        values = jnp.concatenate([r[...] for r in grads], axis=0)
        out[0] = lax.dot_general(
            rows, values, FIRST_DIMS, preferred_element_type=F32
        ).astype(BF)


def weight_grads(x, gates, ups):
    pieces, _, feat = x[0].shape
    hidden = gates[0].shape[1]
    total = sum(v.shape[1] for v in x)
    g_specs = [pl.BlockSpec(v.shape, lambda f: (0, 0)) for v in gates]
    o_spec = pl.BlockSpec((1, feat, hidden), lambda f: (0, f, 0))
    out = jax.ShapeDtypeStruct((1, pieces * feat, hidden), BF)
    return pl.pallas_call(
        functools.partial(weights_kernel, len(x)),
        grid=(pieces,),
        in_specs=[pl.BlockSpec((1,) + v.shape[1:], lambda f: (f, 0, 0)) for v in x]
        + g_specs * 2,
        out_specs=(o_spec, o_spec),
        out_shape=(out, out),
        compiler_params=params("arbitrary"),
        cost_estimate=cost(4 * total * pieces * feat * hidden, 4 * pieces * feat * hidden),
        name="weight_grads",
    )(*x, *gates, *ups)


def scatter_kernel(onehot, rows, out):
    rows = rows[...].reshape(onehot.shape[0], out.shape[1])
    value = lax.dot_general(onehot[...], rows, FIRST_DIMS, preferred_element_type=F32)
    out[...] = value.astype(BF)


def scatter(onehot, values):
    rows, tokens = onehot.shape
    feat = values.shape[2]
    return pl.pallas_call(
        scatter_kernel,
        out_shape=jax.ShapeDtypeStruct((tokens, feat), BF),
        compiler_params=params(limit=16),
        cost_estimate=cost(2 * rows * tokens * feat, 2 * rows * tokens + 4 * tokens * feat),
        name="scatter",
    )(onehot, values)


def together(*groups):
    flat = lax.optimization_barrier([v for g in groups for v in g])
    out = []
    for g in groups:
        out.append(flat[: len(g)])
        flat = flat[len(g) :]
    return out


FOUR = 4
TWO_ON = [(i, (i + 2) % FOUR) for i in range(FOUR)]
PAIRS = [(i, i ^ 1) for i in range(FOUR)]
MIDDLE = [(1, 2), (2, 1)]
OUTWARD = [(1, 0), (2, 3)]
INWARD = [(0, 1), (3, 2)]


def send(value, pairs):
    return lax.ppermute(value, "dp", pairs)


def shift(n, k):
    return [(i, (i + k) % n) for i in range(n)]


def origin(n, block, me):
    return me ^ (0, 2, 1, 3)[block] if n == FOUR else (me - block) % n


class Steps:
    def __init__(self, value):
        self.right = [value]
        self.left = [value]

    def step(self):
        n = lax.axis_size("dp")
        s = len(self.right)
        right, left = self.right[-1], self.left[-1]
        self.right.append(send(right, [(i, i + 1) for i in range(s - 1, n - 1)]))
        self.left.append(send(left, [(i, i - 1) for i in range(1, n - s + 1)]))

    @property
    def last(self):
        return [self.right[-1], self.left[-1]]

    @last.setter
    def last(self, values):
        self.right[-1], self.left[-1] = values

    @property
    def got(self):
        return self.right + self.left[1:]

    @staticmethod
    def sources(n):
        def place(me, at):
            return me - at if at <= me else n - 1 + at - me

        return tuple(tuple(place(j, origin(n, k, j)) for j in range(n)) for k in range(n))


class Gather:
    def __init__(self, value):
        self.got = [value]

    def middle(self):
        if lax.axis_size("dp") == FOUR:
            self.got.append(send(self.got[0], MIDDLE))

    def first(self):
        own, n = self.got[0], lax.axis_size("dp")
        if n == FOUR:
            self.got += [send(own, TWO_ON), send(own, PAIRS)]
        else:
            self.got += [send(own, shift(n, k)) for k in range(1, n)]

    def second(self):
        if lax.axis_size("dp") == FOUR:
            self.got.append(send(self.got[2], OUTWARD))

    @staticmethod
    def sources(n):
        if n == FOUR:
            return ((0,) * n, (2,) * n, (3,) * n, (4, 1, 1, 4))
        return tuple((k,) * n for k in range(n))


def add(*values):
    total = values[0].astype(F32)
    for v in values[1:]:
        total = total + v.astype(F32)
    return total.astype(BF)


class Sum:
    def __init__(self, parts):
        self.parts = parts
        self.got = []
        self.sent = []

    def first(self, last=None):
        n = len(self.parts)
        if n == FOUR:
            last = self.parts[3] if last is None else last
            self.got = [send(last, INWARD), send(self.parts[3], MIDDLE)]
        else:
            self.got = [send(self.parts[k], shift(n, n - k)) for k in range(1, n)]

    def second(self):
        if len(self.parts) == FOUR:
            inward, middle = self.got
            self.sent = [add(self.parts[1], inward)]
            self.got = [send(self.sent[0], TWO_ON), send(self.parts[2], PAIRS), middle]

    def result(self):
        return add(self.parts[0], *self.got)


def widen(values, fold):
    pieces, rows, feat = values.shape
    values = values.reshape(pieces // fold, fold, rows, feat)
    values = jnp.swapaxes(values, 1, 2) if fold > 1 else values
    return values.reshape(pieces // fold * rows, fold * feat)


def narrow(values, fold):
    if fold == 1:
        return values
    pieces, rows, feat = values.shape
    values = values.reshape(pieces, rows, fold, feat // fold)
    return jnp.swapaxes(values, 1, 2).reshape(pieces * fold, rows, feat // fold)


def per_device(attn_rows, out_grad, routes, gates, w_gate, w_up, w_down):
    experts = lax.axis_size("expert")
    groups = lax.axis_size("dp")
    own, top = routes.shape
    feat = attn_rows.shape[1]
    capacity = 3 * own // 64
    late = capacity // 3
    first, second = (capacity - late) * experts, late * experts
    rows = first + second
    fold = 128 // math.gcd(feat, 128)
    pieces = experts // fold
    here = lax.axis_index("dp").astype(jnp.int32)
    me = here[None]
    weights = (w_down, w_gate, w_up)

    def exchange(values):
        return lax.all_to_all(values, "expert", split_axis=0, concat_axis=0, tiled=True)

    table = lax.all_gather(label(routes.T, gates.T, experts), "expert", axis=0)
    early, late, coef, onehot = compact(table, attn_rows, out_grad, experts, first, second)
    early = exchange(early)
    coef = lax.dynamic_index_in_dim(coef, lax.axis_index("expert"), 0, keepdims=False)
    (early, coef), (late,) = together([early, coef], [late])
    x = Steps(early[:, :first].reshape(-1, feat))
    dy = Steps(jnp.concatenate([early[:, first:].reshape(-1, feat), coef], axis=0))
    x.step()
    dy.step()
    late = exchange(late)
    x.last, (late,) = together(x.last, [late])
    for _ in range(groups - 3):
        x.step()
        dy.step()
    x.step()
    dy.last, (late,) = together(dy.last, [late])
    two = Gather(late.reshape(-1, feat))
    dy.step()
    two.middle()
    x.last, dy.last, two.got = together(x.last, dy.last, two.got)
    two.first()
    coef_at = experts * first
    coefs = dy.got if fold == 1 else [v[coef_at:] for v in dy.got]
    coef_sources = Steps.sources(groups)

    def run(sources, arrays, start, count, parts_in, after=()):
        if fold > 1:
            size = experts * count * parts_in
            arrays = [
                widen(v[:size].reshape(experts, parts_in * count, feat), fold) for v in arrays
            ]
        at = coef_at if fold == 1 else 0
        x_rows, grads, parts = expert_pass(
            me, sources, arrays, coef_sources, coefs, at, weights, start, count, after
        )
        return x_rows, grads, [narrow(v, fold) for v in parts]

    xs1, grads1, parts1 = run(coef_sources, x.got + dy.got, 0, first, 1)
    last1 = parts1[3 % groups]
    two.got, parts1 = together(two.got, parts1)
    two.second()
    back1 = Sum(parts1)
    back1.first(last1)
    back1.parts = list(back1.parts)
    two.got, back1.parts[2:3] = together(two.got, back1.parts[2:3])
    back1.second()
    xs2, grads2, parts2 = run(
        Gather.sources(groups), two.got, first, second, 2, back1.sent
    )
    last2 = parts2[3 % groups]
    back1.got, parts2 = together(back1.got, parts2)
    back2 = Sum(parts2)
    back2.first(last2)
    g_gate, g_up = weight_grads([xs1, xs2], *[list(pair) for pair in zip(grads1, grads2)])
    back2.second()
    total = jnp.concatenate([back1.result(), back2.result()], axis=1)
    return scatter(onehot, exchange(total)), g_gate, g_up


def solution(mesh):
    return jax.shard_map(
        per_device,
        mesh=mesh,
        in_specs=(
            P("dp", "expert"),
            P("dp", "expert"),
            P(("dp", "expert"), None),
            P(("dp", "expert"), None),
            P("expert", None, "dp"),
            P("expert", None, "dp"),
            P("expert", "dp", None),
        ),
        out_specs=(P("dp", "expert"), P("expert", None, "dp"), P("expert", None, "dp")),
        check_vma=False,
    )
```
